32 devices in a mesh: grp: 2 (over y), probe: 4 (over z), prof: 2 (over x), sub: 2 (over core).
Axes of the slice: x: 2, y: 2, z: 4, core: 2. Of those that a mesh axis runs over, the one named last changes fastest.
Arguments:
- signal: float32 [8192, 4096], P(('grp', 'probe', 'sub'), 'prof'), parts along dimension 0, may hold values from -32 to 32, as said below
- jump_sizes: float32 [8192, 4096], P(('grp', 'probe', 'sub'), 'prof'), parts along dimension 0, may hold values from -95 to 95
- thresholds: float32 [8192], P(('grp', 'probe', 'sub')), parts along dimension 0, may hold values from 2 to 40
Outputs:
- new_jumps: float32 [8192, 4096], P(('grp', 'probe', 'sub'), 'prof'), parts along dimension 0
The draws below stay inside these ranges and needn't reach their ends.
There are 2 independent parts, one for each index of `grp`. The reference program is written for one: setup_inputs(seed, part) draws one part's arguments, and reference() takes and returns one part's arrays. A program takes and returns all parts, laid end to end along the dimension named above; each array names one. Nothing has to cross between parts.
Inputs may be any that keep to these rules, and one draw needn't show every extreme that they name: `signal`: measurements of one profile share a scale.
All inputs are finite; a program needn't handle non-finite values.
Results may differ from the reference program's by a relative error of at most 0.0001.
Values sent between devices are 32-bit elements; how exact they have to be, the bound alone decides.
No kernel may reach another device: no remote copies, remote signals or barrier semaphores. Data moves between devices by JAX's collectives and lax.ppermute only.
A program may use at most 64 MiB of HBM per device.

```python
import math
import jax
import jax.numpy as jnp
from jax import lax

P_SIZE = 4096
ROWS_DEV = 512
ITERS = 8
PROBES = 4096


def column_scales(key):
    ramp = jnp.arange(P_SIZE, dtype=jnp.float32) / P_SIZE
    jitter = jax.random.uniform(key, (P_SIZE,), jnp.float32, 0.7, 1.4)
    return 0.5 * jnp.power(10.0, ramp) * jitter


def draw_signal(key, part):
    key_scale, key_offset, key_noise, key_level, key_break = jax.random.split(jax.random.fold_in(key, 11), 5)
    scales = column_scales(key_scale)
    position = (jnp.arange(PROBES, dtype=jnp.float32) + 0.5) / PROBES
    columns = (jnp.arange(P_SIZE, dtype=jnp.float32) + 0.5) / P_SIZE
    breaks = 0.1 + 0.8 * columns + jax.random.uniform(key_break, (P_SIZE,), jnp.float32, -0.05, 0.05)
    offsets = 0.5 * jax.random.truncated_normal(key_offset, -2.0, 2.0, (P_SIZE,), jnp.float32)
    levels = 0.6 * jax.random.truncated_normal(key_level, -2.0, 2.0, (P_SIZE,), jnp.float32)
    noise = jax.random.truncated_normal(key_noise, -2.0, 2.0, (PROBES, P_SIZE), jnp.float32)
    stepped_level = jnp.where(position[:, None] > breaks[None, :], levels[None, :], 0.0)
    return (scales[None, :] * (offsets[None, :] + stepped_level + noise)).astype(jnp.float32)


def draw_jump_sizes(key, part):
    key_scale, key_rows, key_mean, key_noise = jax.random.split(jax.random.fold_in(key, 23), 4)
    scales = column_scales(key_scale)
    within = (jnp.arange(PROBES) % ROWS_DEV).astype(jnp.float32)
    rise = (within + 0.5) / ROWS_DEV
    rough = jax.random.uniform(key_rows, (PROBES,), jnp.float32, 0.0, 1.0)
    row_factor = jnp.exp(jnp.log(0.02) + jnp.log(150.0) * (0.75 * rise + 0.25 * rough))
    means = 0.5 * jax.random.truncated_normal(key_mean, -3.0, 3.0, (P_SIZE,), jnp.float32)
    noise = jax.random.truncated_normal(key_noise, -3.0, 3.0, (PROBES, P_SIZE), jnp.float32)
    return (row_factor[:, None] * scales[None, :] * (means[None, :] + noise)).astype(jnp.float32)


def shard_levels(rng, dims, cuts, smallest, largest):
    def one(dim, parts):
        steps = jax.random.uniform(jax.random.fold_in(jax.random.fold_in(rng, 6), dim), (parts,), jnp.float32, smallest / len(cuts), largest / len(cuts))
        return jnp.repeat(jnp.exp(steps), dims[dim] // parts).reshape((-1,) + (1,) * (len(dims) - dim - 1))

    level = one(*cuts[0])
    for cut in cuts[1:]:
        level = level * one(*cut)
    return level


def setup_inputs(seed: int = 0, part: int = 0) -> dict:
    splits = jax.random.split(jax.random.key(seed), 4)
    part_keys = jax.random.split(jax.random.fold_in(splits[3], part), 4)
    signal = draw_signal(jax.random.fold_in(jax.random.fold_in(splits[3], part), 71), part)
    jump_sizes = draw_jump_sizes(jax.random.fold_in(jax.random.fold_in(splits[3], part), 71), part)
    thresholds = jnp.clip(jnp.exp(math.log(40.0) - 2.9957323 * jax.random.uniform(part_keys[2], (PROBES,), jnp.float32) ** shard_levels(part_keys[2], (PROBES,), ((0, 8),), -0.2, 0.2)), 2.0, 40.0)
    return {"signal": signal, "jump_sizes": jump_sizes, "thresholds": thresholds}


step_length = 2.0

def reference(signal, jump_sizes, thresholds):
    inverse_count = 1.0 / PROBES
    jumps = jump_sizes
    for iteration in range(ITERS):
        fitted = jnp.cumsum(jumps, axis=0) * inverse_count
        residual = signal - fitted
        gradient = jnp.flip(jnp.cumsum(jnp.flip(residual, 0), axis=0), 0) * inverse_count
        stepped = jumps + step_length * gradient
        squares = lax.optimization_barrier(jnp.sum(stepped * stepped, axis=1))
        factor = jnp.maximum(0.0, 1.0 - thresholds / jnp.sqrt(squares + 1e-06))
        jumps = stepped * factor[:, None]
    return jumps
```

```python
import functools

import jax
import jax.numpy as jnp
from jax import lax
from jax.experimental import pallas as pl
from jax.experimental.pallas import tpu as pltpu
from jax.sharding import PartitionSpec as P

ITERS = 8
STEP_LENGTH = 2.0
LANES = 128
SUBLANES = 8
VMEM_LIMIT = 16 * 1024 * 1024


def tiles(cols):
    return [slice(j * LANES, (j + 1) * LANES) for j in range(cols // LANES)]


def row_weights():
    return (SUBLANES - 1 - lax.broadcasted_iota(jnp.int32, (SUBLANES, LANES), 0)).astype(jnp.float32)


def finish_sums(depth, total, weighted, totals_ref, weighted_ref, message_ref, cols):
    weights = row_weights() * float(depth)
    for j, c in enumerate(tiles(cols)):
        totals_ref[:, c] = total[j]
        weighted_ref[:, c] = weighted[j]
        message_ref[0:1, c] = jnp.sum(total[j], axis=0, keepdims=True)
        message_ref[1:2, c] = jnp.sum(weights * total[j] + weighted[j], axis=0, keepdims=True)


def begin_kernel(beta, count, signal_hbm, jumps_hbm, state_ref, const_ref, minus_ref, totals_ref, weighted_ref,
                 message_ref, sems):
    depth, _, cols = state_ref.shape
    cs = tiles(cols)
    parts = depth // SUBLANES

    def copies(part):
        for a, (src, dst) in enumerate(((signal_hbm, const_ref), (jumps_hbm, state_ref))):
            for s in range(SUBLANES):
                yield pltpu.make_async_copy(
                    src.at[pl.ds(s * depth + part * SUBLANES, SUBLANES), :],
                    dst.at[pl.ds(part * SUBLANES, SUBLANES), s, :],
                    sems.at[a, part, s],
                )

    for part in reversed(range(parts)):
        for copy in copies(part):
            copy.start()
    zero = jnp.zeros((SUBLANES, LANES), jnp.float32)
    carry = ([zero] * len(cs), [zero] * len(cs), [zero] * len(cs))
    for part in reversed(range(parts)):
        for copy in copies(part):
            copy.wait()

        def step(i, carry, part=part):
            suffix, total, weighted = (list(x) for x in carry)
            k = part * SUBLANES + SUBLANES - 1 - i
            weight = (depth - k).astype(jnp.float32)
            for j, c in enumerate(cs):
                suffix[j] = suffix[j] + const_ref[k, :, c]
                const_ref[k, :, c] = suffix[j] * beta
                jump = state_ref[k, :, c]
                total[j] = total[j] + jump
                weighted[j] = weighted[j] + jump * weight
            return suffix, total, weighted

        carry = lax.fori_loop(0, SUBLANES, step, carry)
    suffix, total, weighted = carry
    for j, c in enumerate(cs):
        minus = suffix[j] * -count
        minus_ref[:, c] = minus
        weighted[j] = weighted[j] + minus
    finish_sums(depth, total, weighted, totals_ref, weighted_ref, message_ref, cols)


def shrink(own_ref, other_ref, limits_ref, factor_ref):
    squares = own_ref[...] + other_ref[...]
    factor = jnp.maximum(0.0, 1.0 - limits_ref[...] / jnp.sqrt(squares + 1e-06))
    rows = factor.shape[1]
    spread = jnp.broadcast_to(factor, (LANES, rows)).T
    factor_ref[...] = spread.reshape(factor_ref.shape)


def sums_kernel(own_ref, other_ref, limits_ref, state_ref, minus_ref, factor_ref, totals_ref, weighted_ref, message_ref):
    depth, _, cols = state_ref.shape
    cs = tiles(cols)
    shrink(own_ref, other_ref, limits_ref, factor_ref)

    def step(k, carry):
        total, weighted = (list(x) for x in carry)
        factor = factor_ref[k]
        for j, c in enumerate(cs):
            total[j] = total[j] + state_ref[k, :, c] * factor
            weighted[j] = weighted[j] + total[j]
        return total, weighted

    zero = jnp.zeros((SUBLANES, LANES), jnp.float32)
    total, weighted = lax.fori_loop(0, depth, step, ([zero] * len(cs), [minus_ref[:, c] for c in cs]), unroll=2)
    finish_sums(depth, total, weighted, totals_ref, weighted_ref, message_ref, cols)


def prefix_rows(x, sublane):
    for shift in (1, 2, 4):
        x = x + jnp.where(sublane >= shift, pltpu.roll(x, shift, 0), 0.0)
    return x


def suffix_rows(x, sublane):
    for shift in (1, 2, 4):
        x = x + jnp.where(sublane < SUBLANES - shift, pltpu.roll(x, SUBLANES - shift, 0), 0.0)
    return x


def inner_kernel(alpha, chips, scaled, state_ref, const_ref, factor_ref, totals_ref, weighted_ref, message_ref,
                 sibling_ref, inner_ref, slope_ref, base_ref):
    depth, _, cols = state_ref.shape
    rows = float(depth * SUBLANES)
    cs = tiles(cols)
    chip, core = lax.axis_index("probe"), lax.axis_index("sub")
    first = (core == 0).astype(jnp.float32)
    later = (chips - 1 - chip).astype(jnp.float32) * (2.0 * rows)
    sublane = lax.broadcasted_iota(jnp.int32, (SUBLANES, LANES), 0)
    weights = row_weights() * float(depth)

    def step(i, carry):
        running, double = (list(x) for x in carry)
        k = depth - 1 - i
        if scaled:
            factor = factor_ref[k]
        for j, c in enumerate(cs):
            jump = state_ref[k, :, c]
            if scaled:
                jump = jump * factor
            double[j] = double[j] + running[j]
            inner_ref[k, :, c] = jump + const_ref[k, :, c] - double[j]
            running[j] = running[j] - jump * alpha
        return running, double

    zero = jnp.zeros((SUBLANES, LANES), jnp.float32)
    lax.fori_loop(0, depth, step, ([totals_ref[:, c] * alpha for c in cs], [zero] * len(cs)), unroll=2)

    for c in cs:
        total = totals_ref[:, c]
        before = jnp.where(sublane >= 1, pltpu.roll(prefix_rows(total, sublane), 1, 0), 0.0)
        chunk = before * float(depth) + weighted_ref[:, c]
        after = jnp.where(
            sublane < SUBLANES - 1, pltpu.roll(suffix_rows(chunk, sublane), SUBLANES - 1, 0), 0.0
        )
        own, sibling = message_ref[0:1, c], sibling_ref[0:1, c]
        lower = first * own + (1.0 - first) * sibling
        shift = (1.0 - first) * lower
        base = later * (own + sibling) + first * (rows * lower + sibling_ref[1:2, c])
        slope_ref[:, c] = alpha * (before + shift)
        base_ref[:, c] = alpha * (after + base + weights * shift)


def outer_kernel(alpha, chips, offsets, inner_ref, slope_ref, base_ref, *refs):
    received, (state_ref, squares_ref, wide_ref) = refs[: len(offsets)], refs[len(offsets) :]
    depth, _, cols = inner_ref.shape
    rows = float(depth * SUBLANES)
    cs = tiles(cols)
    chip, core = lax.axis_index("probe"), lax.axis_index("sub")
    later = (chips - 1 - chip).astype(jnp.float32) * (2.0 * rows) + (core == 0).astype(jnp.float32) * rows
    weights = row_weights() * float(depth) + later
    earlier = [(jnp.bitwise_xor(chip, k) < chip).astype(jnp.float32) for k in offsets]

    slope, value = [], []
    for c in cs:
        above = sum(e * ref[:, c] for e, ref in zip(earlier, received))
        below = sum((1.0 - e) * ref[:, c] for e, ref in zip(earlier, received))
        above, below = above * alpha, below * alpha
        slope.append(slope_ref[:, c] + above)
        value.append(base_ref[:, c] + below + weights * above + slope[-1])

    def step(i, value):
        value = list(value)
        k = depth - 1 - i
        squares = []
        for j, c in enumerate(cs):
            stepped = inner_ref[k, :, c] - value[j]
            state_ref[k, :, c] = stepped
            value[j] = value[j] + slope[j]
            squares.append(stepped * stepped)
        while len(squares) > 1:
            squares = [a + b for a, b in zip(squares[::2], squares[1::2])]
        wide_ref[pl.ds(pl.multiple_of(k * SUBLANES, SUBLANES), SUBLANES), :] = squares[0]
        return value

    lax.fori_loop(0, depth, step, value, unroll=2)
    ones = jnp.ones((SUBLANES, LANES), jnp.float32)
    squares = lax.dot_general(
        ones, wide_ref[...], (((1,), (1,)), ((), ())), precision=lax.Precision.HIGHEST,
        preferred_element_type=jnp.float32,
    )
    squares_ref[...] = squares[0:1, :]


def end_kernel(own_ref, other_ref, limits_ref, state_ref, out_hbm, factor_ref, jumps_ref, sems):
    depth, _, cols = state_ref.shape
    cs = tiles(cols)
    shrink(own_ref, other_ref, limits_ref, factor_ref)
    copies = []
    for part in range(depth // SUBLANES):

        def step(i, carry, part=part):
            k = part * SUBLANES + i
            factor = factor_ref[k]
            for c in cs:
                jumps_ref[k, :, c] = state_ref[k, :, c] * factor
            return carry

        lax.fori_loop(0, SUBLANES, step, 0, unroll=2)
        for s in range(SUBLANES):
            copy = pltpu.make_async_copy(
                jumps_ref.at[pl.ds(part * SUBLANES, SUBLANES), s, :],
                out_hbm.at[pl.ds(s * depth + part * SUBLANES, SUBLANES), :],
                sems.at[part, s],
            )
            copy.start()
            copies.append(copy)
    for copy in copies:
        copy.wait()


def vmem(*shape):
    return pltpu.VMEM(shape, jnp.float32)


def call(kernel, name, operands, outs, kept=(), scratch=(), aliases=None, hbm=(), hbm_out=False):
    in_vmem = pl.BlockSpec(memory_space=pltpu.VMEM)
    in_hbm = pl.BlockSpec(memory_space=pl.ANY)
    operands = [
        pltpu.with_memory_space_constraint(x, pltpu.VMEM) if i in kept else x for i, x in enumerate(operands)
    ]
    return pl.pallas_call(
        kernel,
        out_shape=outs,
        in_specs=[in_hbm if i in hbm else in_vmem for i in range(len(operands))],
        out_specs=in_hbm if hbm_out else [in_vmem] * len(outs),
        scratch_shapes=scratch,
        input_output_aliases=aliases or {},
        compiler_params=pltpu.CompilerParams(vmem_limit_bytes=VMEM_LIMIT),
        name=name,
    )(*operands)


def local(mesh, signal, jump_sizes, thresholds):
    rows, cols = signal.shape
    chips, cores, halves = mesh.shape["probe"], mesh.shape["sub"], mesh.shape["prof"]
    depth = rows // SUBLANES
    count = float(rows * chips * cores)
    alpha, beta = STEP_LENGTH / (count * count), STEP_LENGTH / count
    chip, core = lax.axis_index("probe"), lax.axis_index("sub")
    offsets = tuple(reversed(range(1, chips)))
    swap = [(0, 1), (1, 0)]
    routes = {
        k: [(z * 2 + c, (z ^ k) * 2 + 1 - c) for z in range(chips) for c in range(2)] for k in offsets
    }
    limits = thresholds.reshape(SUBLANES, depth).T.reshape(1, rows)

    block = vmem(depth, SUBLANES, cols)
    strip, line, pair = vmem(SUBLANES, cols), vmem(1, rows), vmem(2, cols)
    spread = vmem(depth, SUBLANES, LANES)

    state, const, minus, totals, weighted, message = call(
        functools.partial(begin_kernel, beta, count), "begin", [signal, jump_sizes],
        [block, block, strip, strip, strip, pair], hbm=(0, 1),
        scratch=[pltpu.SemaphoreType.DMA((2, depth // SUBLANES, SUBLANES))],
    )
    factor = None
    for iteration in range(ITERS):
        if iteration:
            factor, totals, weighted, message = call(
                sums_kernel, "sums", [own, other, limits, state, minus], [spread, strip, strip, pair], kept=(3, 4)
            )
        sibling = lax.ppermute(message, "sub", swap)
        both = message + sibling
        lower = jnp.where(core == 0, message[0:1], sibling[0:1])
        upward = both[0:1]
        later = (chips - 1 - chip).astype(jnp.float32) * (2.0 * rows)
        downward = both[1:2] + float(rows) * lower + later * upward
        received = [
            lax.ppermute(jnp.where(jnp.bitwise_xor(chip, k) > chip, upward, downward), ("probe", "sub"), routes[k])
            for k in offsets
        ]
        scaled = factor is not None
        inner, slope, base = call(
            functools.partial(inner_kernel, alpha, chips, scaled), "inner",
            [state, const, factor if scaled else minus, totals, weighted, message, sibling],
            [block, strip, strip], kept=(0, 1, 2, 3, 4), aliases={0: 0},
        )
        state, own = call(
            functools.partial(outer_kernel, alpha, chips, offsets), "outer", [inner, slope, base, *received],
            [block, line], kept=(0, 1, 2), aliases={0: 0}, scratch=[vmem(rows, LANES)],
        )
        if halves == 2:
            other = lax.ppermute(own, "prof", swap)
        else:
            own, other = lax.psum(own, "prof"), jnp.zeros_like(own)
    return call(
        end_kernel, "finish", [own, other, limits, state], jax.ShapeDtypeStruct((rows, cols), jnp.float32), kept=(3,),
        hbm_out=True,
        scratch=[spread, block, pltpu.SemaphoreType.DMA((depth // SUBLANES, SUBLANES))],
    )


def solution(mesh):
    spec = P(("grp", "probe", "sub"), "prof")
    return jax.shard_map(
        functools.partial(local, mesh),
        mesh=mesh,
        in_specs=(spec, spec, P(("grp", "probe", "sub"))),
        out_specs=spec,
        check_vma=False,
    )
```

```python
import functools

import jax
import jax.numpy as jnp
from jax import lax
from jax.experimental import pallas as pl
from jax.experimental.pallas import tpu as pltpu
from jax.sharding import PartitionSpec as P

ITERS = 8
STEP_LENGTH = 2.0
LANES = 128
SUBLANES = 8
VMEM_LIMIT = 16 * 1024 * 1024
WIDTH, BATCH = 8, 4
OUTER_WIDTH, OUTER_BATCH = 8, 4


def tiles(cols):
    return [slice(j * LANES, (j + 1) * LANES) for j in range(cols // LANES)]


def groups(cols, width):
    cs = tiles(cols)
    return [cs[g : g + width] for g in range(0, len(cs), width)]


def row_weights():
    return (SUBLANES - 1 - lax.broadcasted_iota(jnp.int32, (SUBLANES, LANES), 0)).astype(jnp.float32)


def finish_sums(depth, total, weighted, totals_ref, weighted_ref, message_ref, cols):
    weights = row_weights() * float(depth)
    for j, c in enumerate(tiles(cols)):
        totals_ref[:, c] = total[j]
        weighted_ref[:, c] = weighted[j]
        message_ref[0:1, c] = jnp.sum(total[j], axis=0, keepdims=True)
        message_ref[1:2, c] = jnp.sum(weights * total[j] + weighted[j], axis=0, keepdims=True)


def begin_kernel(chips, beta, count, signal_hbm, jumps_hbm, thresholds_ref, state_ref, const_ref, minus_ref, totals_ref,
                 weighted_ref, message_ref, limits_ref, marks_ref, sems):
    depth, _, cols = state_ref.shape
    cs = tiles(cols)
    parts = depth // SUBLANES

    def copies(part):
        for a, (src, dst) in enumerate(((signal_hbm, const_ref), (jumps_hbm, state_ref))):
            for s in range(SUBLANES):
                yield pltpu.make_async_copy(
                    src.at[pl.ds(s * depth + part * SUBLANES, SUBLANES), :],
                    dst.at[pl.ds(part * SUBLANES, SUBLANES), s, :],
                    sems.at[a, part, s],
                )

    for part in reversed(range(parts)):
        for copy in copies(part):
            copy.start()

    rows = depth * SUBLANES
    source = lax.broadcasted_iota(jnp.int32, (rows, rows), 0)
    target = lax.broadcasted_iota(jnp.int32, (rows, rows), 1)
    chosen = jnp.where(source == (target % SUBLANES) * depth + target // SUBLANES, 1.0, 0.0)
    limits_ref[...] = lax.dot_general(
        jnp.broadcast_to(thresholds_ref[...], (SUBLANES, rows)), chosen, (((1,), (0,)), ((), ())),
        precision=lax.Precision.HIGHEST, preferred_element_type=jnp.float32,
    )[0:1, :]
    chip, core = lax.axis_index("probe"), lax.axis_index("sub")
    later = (chips - 1 - chip).astype(jnp.float32) * (2.0 * rows)
    marks = [(core == 0).astype(jnp.float32), later]
    marks += [(jnp.bitwise_xor(chip, k) > chip).astype(jnp.float32) for k in range(1, chips)]
    for i, mark in enumerate(marks):
        marks_ref[i : i + 1, :] = jnp.full((1, cols), mark, jnp.float32)

    zero = jnp.zeros((SUBLANES, LANES), jnp.float32)
    carry = ([zero] * len(cs), [zero] * len(cs), [zero] * len(cs))
    for part in reversed(range(parts)):
        for copy in copies(part):
            copy.wait()

        def step(i, carry, part=part):
            suffix, total, weighted = (list(x) for x in carry)
            k = part * SUBLANES + SUBLANES - 1 - i
            weight = (depth - k).astype(jnp.float32)
            for j, c in enumerate(cs):
                jump = state_ref[k, :, c]
                total[j] = total[j] + jump
                weighted[j] = weighted[j] + jump * weight
                suffix[j] = suffix[j] + const_ref[k, :, c]
            for j, c in enumerate(cs):
                const_ref[k, :, c] = suffix[j] * beta
            return suffix, total, weighted

        carry = lax.fori_loop(0, SUBLANES, step, carry)
    suffix, total, weighted = carry
    for j, c in enumerate(cs):
        minus = suffix[j] * -count
        minus_ref[:, c] = minus
        weighted[j] = weighted[j] + minus
    finish_sums(depth, total, weighted, totals_ref, weighted_ref, message_ref, cols)


def shrink(own_ref, other_ref, limits_ref, factor_ref):
    squares = own_ref[...] + other_ref[...]
    factor = jnp.maximum(0.0, 1.0 - limits_ref[...] / jnp.sqrt(squares + 1e-06))
    rows = factor.shape[1]
    spread = jnp.broadcast_to(factor, (LANES, rows)).T
    factor_ref[...] = spread.reshape(factor_ref.shape)


def sums_kernel(own_ref, other_ref, limits_ref, state_ref, minus_ref, factor_ref, totals_ref, weighted_ref, message_ref):
    depth, _, cols = state_ref.shape
    cs = tiles(cols)
    shrink(own_ref, other_ref, limits_ref, factor_ref)

    def step(k, carry):
        total, weighted = (list(x) for x in carry)
        factor = factor_ref[k]
        for j, c in enumerate(cs):
            total[j] = total[j] + state_ref[k, :, c] * factor
            weighted[j] = weighted[j] + total[j]
        return total, weighted

    zero = jnp.zeros((SUBLANES, LANES), jnp.float32)
    total, weighted = lax.fori_loop(0, depth, step, ([zero] * len(cs), [minus_ref[:, c] for c in cs]), unroll=2)
    finish_sums(depth, total, weighted, totals_ref, weighted_ref, message_ref, cols)


def prefix_rows(x, sublane):
    for shift in (1, 2, 4):
        x = x + jnp.where(sublane >= shift, pltpu.roll(x, shift, 0), 0.0)
    return x


def suffix_rows(x, sublane):
    for shift in (1, 2, 4):
        x = x + jnp.where(sublane < SUBLANES - shift, pltpu.roll(x, SUBLANES - shift, 0), 0.0)
    return x


def inner_kernel(alpha, chips, scaled, state_ref, const_ref, factor_ref, totals_ref, weighted_ref, message_ref,
                 sibling_ref, inner_ref, slope_ref, base_ref):
    depth, _, cols = state_ref.shape
    rows = float(depth * SUBLANES)
    cs = tiles(cols)
    chip, core = lax.axis_index("probe"), lax.axis_index("sub")
    first = (core == 0).astype(jnp.float32)
    later = (chips - 1 - chip).astype(jnp.float32) * (2.0 * rows)
    sublane = lax.broadcasted_iota(jnp.int32, (SUBLANES, LANES), 0)
    weights = row_weights() * float(depth)

    zero = jnp.zeros((SUBLANES, LANES), jnp.float32)
    for group in groups(cols, WIDTH):

        def step(i, carry, group=group):
            running, double = (list(x) for x in carry)
            start = depth - (i + 1) * BATCH
            results = []
            for k in reversed([start + q for q in range(BATCH)]):
                factor = factor_ref[k] if scaled else None
                for j, c in enumerate(group):
                    jump = state_ref[k, :, c]
                    if scaled:
                        jump = jump * factor
                    double[j] = double[j] + running[j]
                    results.append((k, c, jump + const_ref[k, :, c] - double[j]))
                    running[j] = running[j] - jump * alpha
            for k, c, value in results:
                inner_ref[k, :, c] = value
            return running, double

        lax.fori_loop(
            0, depth // BATCH, step, ([totals_ref[:, c] * alpha for c in group], [zero] * len(group))
        )

    for c in cs:
        total = totals_ref[:, c]
        before = jnp.where(sublane >= 1, pltpu.roll(prefix_rows(total, sublane), 1, 0), 0.0)
        chunk = before * float(depth) + weighted_ref[:, c]
        after = jnp.where(
            sublane < SUBLANES - 1, pltpu.roll(suffix_rows(chunk, sublane), SUBLANES - 1, 0), 0.0
        )
        own, sibling = message_ref[0:1, c], sibling_ref[0:1, c]
        lower = first * own + (1.0 - first) * sibling
        shift = (1.0 - first) * lower
        base = later * (own + sibling) + first * (rows * lower + sibling_ref[1:2, c])
        slope_ref[:, c] = alpha * (before + shift)
        base_ref[:, c] = alpha * (after + base + weights * shift)


def outer_kernel(alpha, chips, offsets, inner_ref, slope_ref, base_ref, *refs):
    received, (state_ref, squares_ref, wide_ref) = refs[: len(offsets)], refs[len(offsets) :]
    depth, _, cols = inner_ref.shape
    rows = float(depth * SUBLANES)
    chip, core = lax.axis_index("probe"), lax.axis_index("sub")
    later = (chips - 1 - chip).astype(jnp.float32) * (2.0 * rows) + (core == 0).astype(jnp.float32) * rows
    weights = row_weights() * float(depth) + later
    earlier = [(jnp.bitwise_xor(chip, k) < chip).astype(jnp.float32) for k in offsets]

    for g, group in enumerate(groups(cols, OUTER_WIDTH)):
        slope, value = [], []
        for c in group:
            above = sum(e * ref[:, c] for e, ref in zip(earlier, received))
            below = sum((1.0 - e) * ref[:, c] for e, ref in zip(earlier, received))
            above, below = above * alpha, below * alpha
            slope.append(slope_ref[:, c] + above)
            value.append(base_ref[:, c] + below + weights * above + slope[-1])

        def step(i, value, g=g, group=group, slope=slope):
            value = list(value)
            start = depth - (i + 1) * OUTER_BATCH
            results, sums = [], []
            for k in reversed([start + q for q in range(OUTER_BATCH)]):
                squares = []
                for j, c in enumerate(group):
                    stepped = inner_ref[k, :, c] - value[j]
                    value[j] = value[j] + slope[j]
                    results.append((k, c, stepped))
                    squares.append(stepped * stepped)
                while len(squares) > 1:
                    squares = [a + b for a, b in zip(squares[::2], squares[1::2])]
                sums.append((k, squares[0]))
            for k, c, stepped in results:
                state_ref[k, :, c] = stepped
            for k, total in sums:
                wide_ref[pl.ds(pl.multiple_of(k * SUBLANES, SUBLANES), SUBLANES), g * LANES : (g + 1) * LANES] = total
            return value

        lax.fori_loop(0, depth // OUTER_BATCH, step, value)

    ones = jnp.ones((SUBLANES, wide_ref.shape[1]), jnp.float32)
    squares = lax.dot_general(
        ones, wide_ref[...], (((1,), (1,)), ((), ())), precision=lax.Precision.HIGHEST,
        preferred_element_type=jnp.float32,
    )
    squares_ref[...] = squares[0:1, :]


def end_kernel(own_ref, other_ref, limits_ref, state_ref, out_hbm, factor_ref, jumps_ref, sems):
    depth, _, cols = state_ref.shape
    cs = tiles(cols)
    shrink(own_ref, other_ref, limits_ref, factor_ref)
    copies = []
    for part in range(depth // SUBLANES):

        def step(i, carry, part=part):
            k = part * SUBLANES + i
            factor = factor_ref[k]
            values = [state_ref[k, :, c] * factor for c in cs]
            for c, value in zip(cs, values):
                jumps_ref[k, :, c] = value
            return carry

        lax.fori_loop(0, SUBLANES, step, 0, unroll=2)
        for s in range(SUBLANES):
            copy = pltpu.make_async_copy(
                jumps_ref.at[pl.ds(part * SUBLANES, SUBLANES), s, :],
                out_hbm.at[pl.ds(s * depth + part * SUBLANES, SUBLANES), :],
                sems.at[part, s],
            )
            copy.start()
            copies.append(copy)
    for copy in copies:
        copy.wait()


def vmem(*shape):
    return pltpu.VMEM(shape, jnp.float32)


def call(kernel, name, operands, outs, kept=(), scratch=(), aliases=None, hbm=(), hbm_out=False):
    in_vmem = pl.BlockSpec(memory_space=pltpu.VMEM)
    in_hbm = pl.BlockSpec(memory_space=pltpu.HBM)
    operands = [
        pltpu.with_memory_space_constraint(x, pltpu.VMEM if i in kept else pltpu.HBM) if i in kept or i in hbm else x
        for i, x in enumerate(operands)
    ]
    return pl.pallas_call(
        kernel,
        out_shape=outs,
        in_specs=[in_hbm if i in hbm else in_vmem for i in range(len(operands))],
        out_specs=in_hbm if hbm_out else [in_vmem] * len(outs),
        scratch_shapes=scratch,
        input_output_aliases=aliases or {},
        compiler_params=pltpu.CompilerParams(vmem_limit_bytes=VMEM_LIMIT),
        name=name,
    )(*operands)


def local(mesh, signal, jump_sizes, thresholds):
    rows, cols = signal.shape
    chips, cores, halves = mesh.shape["probe"], mesh.shape["sub"], mesh.shape["prof"]
    depth = rows // SUBLANES
    count = float(rows * chips * cores)
    alpha, beta = STEP_LENGTH / (count * count), STEP_LENGTH / count
    offsets = tuple(reversed(range(1, chips)))
    swap = [(0, 1), (1, 0)]
    routes = {
        k: [(z * 2 + c, (z ^ k) * 2 + 1 - c) for z in range(chips) for c in range(2)] for k in offsets
    }

    block = vmem(depth, SUBLANES, cols)
    strip, line, pair = vmem(SUBLANES, cols), vmem(1, rows), vmem(2, cols)
    spread = vmem(depth, SUBLANES, LANES)

    state, const, minus, totals, weighted, message, limits, marks = call(
        functools.partial(begin_kernel, chips, beta, count), "begin", [signal, jump_sizes, thresholds.reshape(1, rows)],
        [block, block, strip, strip, strip, pair, line, vmem(chips + 1, cols)], hbm=(0, 1),
        scratch=[pltpu.SemaphoreType.DMA((2, depth // SUBLANES, SUBLANES))],
    )
    factor = None
    for iteration in range(ITERS):
        if iteration:
            factor, totals, weighted, message = call(
                sums_kernel, "sums", [own, other, limits, state, minus], [spread, strip, strip, pair], kept=(3, 4)
            )
        sibling = lax.ppermute(message, "sub", swap)
        both = message + sibling
        lower = jnp.where(marks[0:1] > 0.0, message[0:1], sibling[0:1])
        upward = both[0:1]
        downward = both[1:2] + float(rows) * lower + marks[1:2] * upward
        received = [
            lax.ppermute(jnp.where(marks[1 + k : 2 + k] > 0.0, upward, downward), ("probe", "sub"), routes[k])
            for k in offsets
        ]
        scaled = factor is not None
        inner, slope, base = call(
            functools.partial(inner_kernel, alpha, chips, scaled), "inner",
            [state, const, factor if scaled else minus, totals, weighted, message, sibling],
            [block, strip, strip], kept=(0, 1, 2, 3, 4), aliases={0: 0},
        )
        state, own = call(
            functools.partial(outer_kernel, alpha, chips, offsets), "outer", [inner, slope, base, *received],
            [block, line], kept=(0, 1, 2), aliases={0: 0}, scratch=[vmem(rows, LANES * len(groups(cols, OUTER_WIDTH)))],
        )
        if halves == 2:
            other = lax.ppermute(own, "prof", swap)
        else:
            own, other = lax.psum(own, "prof"), jnp.zeros_like(own)
    return call(
        end_kernel, "finish", [own, other, limits, state], jax.ShapeDtypeStruct((rows, cols), jnp.float32), kept=(3,),
        hbm_out=True,
        scratch=[spread, block, pltpu.SemaphoreType.DMA((depth // SUBLANES, SUBLANES))],
    )


def solution(mesh):
    spec = P(("grp", "probe", "sub"), "prof")
    return jax.shard_map(
        functools.partial(local, mesh),
        mesh=mesh,
        in_specs=(spec, spec, P(("grp", "probe", "sub"))),
        out_specs=spec,
        check_vma=False,
    )
```

```python
import functools

import jax
import jax.numpy as jnp
from jax import lax
from jax.experimental import pallas as pl
from jax.experimental.pallas import tpu as pltpu
from jax.sharding import PartitionSpec as P

ITERS = 8
STEP_LENGTH = 2.0
LANES = 128
SUBLANES = 8
VMEM_LIMIT = 16 * 1024 * 1024
WIDTH, BATCH, SUM_BATCH = 8, 4, 8


def tiles(cols):
    return [slice(j * LANES, (j + 1) * LANES) for j in range(cols // LANES)]


def groups(cols, width):
    cs = tiles(cols)
    return [cs[g : g + width] for g in range(0, len(cs), width)]


def row_weights():
    return (SUBLANES - 1 - lax.broadcasted_iota(jnp.int32, (SUBLANES, LANES), 0)).astype(jnp.float32)


def finish_sums(depth, total, weighted, totals_ref, weighted_ref, message_ref, cols):
    weights = row_weights() * float(depth)
    for j, c in enumerate(tiles(cols)):
        totals_ref[:, c] = total[j]
        weighted_ref[:, c] = weighted[j]
        message_ref[0:1, c] = jnp.sum(total[j], axis=0, keepdims=True)
        message_ref[1:2, c] = jnp.sum(weights * total[j] + weighted[j], axis=0, keepdims=True)


def begin_kernel(chips, count, cuts, signal_hbm, jumps_hbm, thresholds_hbm, state_ref, signal_ref, minus_ref, totals_ref,
                 weighted_ref, message_ref, limits_ref, marks_ref, thresholds_ref, sems, limits_sem):
    depth, _, cols = state_ref.shape
    rows = depth * SUBLANES

    def copies(part):
        low, high = cuts[part], cuts[part + 1]
        for a, (src, dst) in enumerate(((jumps_hbm, state_ref), (signal_hbm, signal_ref))):
            for s in range(SUBLANES):
                yield pltpu.make_async_copy(
                    src.at[pl.ds(s * depth + low, high - low), :], dst.at[pl.ds(low, high - low), s, :],
                    sems.at[part, a, s],
                )

    limits_copy = pltpu.make_async_copy(thresholds_hbm, thresholds_ref, limits_sem)
    limits_copy.start()
    for part in range(len(cuts) - 1):
        for copy in copies(part):
            copy.start()

    chip, core = lax.axis_index("probe"), lax.axis_index("sub")
    later = (chips - 1 - chip).astype(jnp.float32) * (2.0 * rows)
    marks = [(core == 0).astype(jnp.float32), later]
    marks += [(jnp.bitwise_xor(chip, k) > chip).astype(jnp.float32) for k in range(1, chips)]
    for i, mark in enumerate(marks):
        marks_ref[i : i + 1, :] = jnp.full((1, cols), mark, jnp.float32)

    limits_copy.wait()
    sublane = lax.broadcasted_iota(jnp.int32, (SUBLANES, LANES), 0)
    lane = lax.broadcasted_iota(jnp.int32, (SUBLANES, LANES), 1)
    limits = jnp.zeros((SUBLANES, LANES), jnp.float32)
    for s in range(SUBLANES):
        tile, offset = divmod(s * depth, LANES)
        line = jnp.broadcast_to(thresholds_ref[0:1, tile * LANES : (tile + 1) * LANES], (SUBLANES, LANES))
        for copy in range(LANES // depth):
            shift = (copy * depth - offset) % LANES
            moved = pltpu.roll(line, shift, 1) if shift else line
            limits = jnp.where((sublane == s) & (lane // depth == copy), moved, limits)
    limits_ref[...] = limits

    zero = jnp.zeros((SUBLANES, LANES), jnp.float32)
    grouped = groups(cols, WIDTH)
    carries = [([zero] * len(group), [zero] * len(group), [zero] * len(group)) for group in grouped]
    for part in range(len(cuts) - 1):
        for copy in copies(part):
            copy.wait()
        for g, group in enumerate(grouped):

            def step(i, carry, group=group, low=cuts[part]):
                total, weighted, signals = (list(x) for x in carry)
                for q in range(BATCH):
                    k = low + i * BATCH + q
                    for j, c in enumerate(group):
                        total[j] = total[j] + state_ref[k, :, c]
                        weighted[j] = weighted[j] + total[j]
                        signals[j] = signals[j] + signal_ref[k, :, c]
                return total, weighted, signals

            carries[g] = lax.fori_loop(0, (cuts[part + 1] - cuts[part]) // BATCH, step, carries[g])
    total, weighted = [], []
    for group, carry in zip(grouped, carries):
        for c, t, w, x in zip(group, *carry):
            minus = x * -count
            minus_ref[:, c] = minus
            total.append(t)
            weighted.append(w + minus)
    finish_sums(depth, total, weighted, totals_ref, weighted_ref, message_ref, cols)


def suffix_kernel(beta, signal_ref, const_ref):
    depth, _, cols = signal_ref.shape
    zero = jnp.zeros((SUBLANES, LANES), jnp.float32)
    for group in groups(cols, WIDTH):

        def step(i, suffix, group=group):
            suffix = list(suffix)
            start = depth - (i + 1) * BATCH
            results = []
            for k in reversed([start + q for q in range(BATCH)]):
                for j, c in enumerate(group):
                    suffix[j] = suffix[j] + signal_ref[k, :, c]
                    results.append((k, c, suffix[j] * beta))
            for k, c, value in results:
                const_ref[k, :, c] = value
            return suffix

        lax.fori_loop(0, depth // BATCH, step, [zero] * len(group))


def shrink(own_ref, other_ref, limits_ref, factor_ref):
    squares = own_ref[...] + other_ref[...]
    factor = jnp.maximum(0.0, 1.0 - limits_ref[...] / jnp.sqrt(squares + 1e-06))
    for k in range(factor_ref.shape[0]):
        factor_ref[k] = jnp.broadcast_to(factor[:, k : k + 1], (SUBLANES, LANES))


def sums_kernel(own_ref, other_ref, limits_ref, state_ref, minus_ref, factor_ref, totals_ref, weighted_ref, message_ref):
    depth, _, cols = state_ref.shape
    shrink(own_ref, other_ref, limits_ref, factor_ref)
    zero = jnp.zeros((SUBLANES, LANES), jnp.float32)
    totals, weights = [], []
    for group in groups(cols, WIDTH):

        def step(i, carry, group=group):
            total, weighted = (list(x) for x in carry)
            for q in range(SUM_BATCH):
                k = i * SUM_BATCH + q
                factor = factor_ref[k]
                for j, c in enumerate(group):
                    total[j] = total[j] + state_ref[k, :, c] * factor
                    weighted[j] = weighted[j] + total[j]
            return total, weighted

        total, weighted = lax.fori_loop(
            0, depth // SUM_BATCH, step, ([zero] * len(group), [minus_ref[:, c] for c in group])
        )
        totals += total
        weights += weighted
    finish_sums(depth, totals, weights, totals_ref, weighted_ref, message_ref, cols)


def prefix_rows(x, sublane):
    for shift in (1, 2, 4):
        x = x + jnp.where(sublane >= shift, pltpu.roll(x, shift, 0), 0.0)
    return x


def suffix_rows(x, sublane):
    for shift in (1, 2, 4):
        x = x + jnp.where(sublane < SUBLANES - shift, pltpu.roll(x, SUBLANES - shift, 0), 0.0)
    return x


def inner_kernel(alpha, chips, scaled, state_ref, const_ref, factor_ref, totals_ref, weighted_ref, message_ref,
                 sibling_ref, inner_ref, slope_ref, base_ref):
    depth, _, cols = state_ref.shape
    rows = float(depth * SUBLANES)
    cs = tiles(cols)
    chip, core = lax.axis_index("probe"), lax.axis_index("sub")
    first = (core == 0).astype(jnp.float32)
    later = (chips - 1 - chip).astype(jnp.float32) * (2.0 * rows)
    sublane = lax.broadcasted_iota(jnp.int32, (SUBLANES, LANES), 0)
    weights = row_weights() * float(depth)

    zero = jnp.zeros((SUBLANES, LANES), jnp.float32)
    for group in groups(cols, WIDTH):

        def step(i, carry, group=group):
            running, double = (list(x) for x in carry)
            start = depth - (i + 1) * BATCH
            results = []
            for k in reversed([start + q for q in range(BATCH)]):
                factor = factor_ref[k] if scaled else None
                for j, c in enumerate(group):
                    jump = state_ref[k, :, c]
                    if scaled:
                        jump = jump * factor
                    double[j] = double[j] + running[j]
                    results.append((k, c, jump + const_ref[k, :, c] - double[j]))
                    running[j] = running[j] - jump * alpha
            for k, c, value in results:
                inner_ref[k, :, c] = value
            return running, double

        lax.fori_loop(
            0, depth // BATCH, step, ([totals_ref[:, c] * alpha for c in group], [zero] * len(group))
        )

    for c in cs:
        total = totals_ref[:, c]
        before = jnp.where(sublane >= 1, pltpu.roll(prefix_rows(total, sublane), 1, 0), 0.0)
        chunk = before * float(depth) + weighted_ref[:, c]
        after = jnp.where(
            sublane < SUBLANES - 1, pltpu.roll(suffix_rows(chunk, sublane), SUBLANES - 1, 0), 0.0
        )
        own, sibling = message_ref[0:1, c], sibling_ref[0:1, c]
        lower = first * own + (1.0 - first) * sibling
        shift = (1.0 - first) * lower
        base = later * (own + sibling) + first * (rows * lower + sibling_ref[1:2, c])
        slope_ref[:, c] = alpha * (before + shift)
        base_ref[:, c] = alpha * (after + base + weights * shift)


def outer_kernel(alpha, chips, offsets, inner_ref, slope_ref, base_ref, *refs):
    received, (state_ref, squares_ref, wide_ref) = refs[: len(offsets)], refs[len(offsets) :]
    depth, _, cols = inner_ref.shape
    rows = float(depth * SUBLANES)
    chip, core = lax.axis_index("probe"), lax.axis_index("sub")
    later = (chips - 1 - chip).astype(jnp.float32) * (2.0 * rows) + (core == 0).astype(jnp.float32) * rows
    weights = row_weights() * float(depth) + later
    earlier = [(jnp.bitwise_xor(chip, k) < chip).astype(jnp.float32) for k in offsets]

    grouped = groups(cols, WIDTH)
    for g, group in enumerate(grouped):
        slope, value = [], []
        for c in group:
            above = sum(e * ref[:, c] for e, ref in zip(earlier, received))
            below = sum((1.0 - e) * ref[:, c] for e, ref in zip(earlier, received))
            above, below = above * alpha, below * alpha
            slope.append(slope_ref[:, c] + above)
            value.append(base_ref[:, c] + below + weights * above + slope[-1])

        def step(i, value, g=g, group=group, slope=slope):
            value = list(value)
            start = depth - (i + 1) * BATCH
            results, sums = [], []
            for k in reversed([start + q for q in range(BATCH)]):
                squares = []
                for j, c in enumerate(group):
                    stepped = inner_ref[k, :, c] - value[j]
                    value[j] = value[j] + slope[j]
                    results.append((k, c, stepped))
                    squares.append(stepped * stepped)
                while len(squares) > 1:
                    squares = [a + b for a, b in zip(squares[::2], squares[1::2])]
                sums.append((k, squares[0]))
            for k, c, stepped in results:
                state_ref[k, :, c] = stepped
            for k, total in sums:
                wide_ref[g, k] = total
            return value

        lax.fori_loop(0, depth // BATCH, step, value, unroll=2)
    lane = lax.broadcasted_iota(jnp.int32, (SUBLANES, LANES), 1)
    parts = []
    for low in range(0, depth, SUBLANES):
        part = jnp.zeros((SUBLANES, LANES), jnp.float32)
        for k in range(low, low + SUBLANES):
            total = jnp.sum(sum(wide_ref[g, k] for g in range(len(grouped))), axis=1, keepdims=True)
            part = jnp.where(lane % depth == k, jnp.broadcast_to(total, part.shape), part)
        parts.append(part)
    squares_ref[...] = sum(parts)


def end_kernel(cuts, own_ref, other_ref, limits_ref, state_ref, out_hbm, factor_ref, jumps_ref, sems):
    depth, _, cols = state_ref.shape
    shrink(own_ref, other_ref, limits_ref, factor_ref)
    copies = []
    for part in range(len(cuts) - 1):
        low, high = cuts[part], cuts[part + 1]
        for group in groups(cols, WIDTH):

            def step(i, carry, low=low, group=group):
                results = []
                for q in range(BATCH):
                    k = low + i * BATCH + q
                    factor = factor_ref[k]
                    results += [(k, c, state_ref[k, :, c] * factor) for c in group]
                for k, c, value in results:
                    jumps_ref[k, :, c] = value
                return carry

            lax.fori_loop(0, (high - low) // BATCH, step, 0)
        for s in range(SUBLANES):
            copy = pltpu.make_async_copy(
                jumps_ref.at[pl.ds(low, high - low), s, :], out_hbm.at[pl.ds(s * depth + low, high - low), :],
                sems.at[part, s],
            )
            copy.start()
            copies.append(copy)
    for copy in copies:
        copy.wait()


def vmem(*shape):
    return pltpu.VMEM(shape, jnp.float32)


def call(kernel, name, operands, outs, kept=(), scratch=(), aliases=None, hbm=(), hbm_out=False):
    in_vmem = pl.BlockSpec(memory_space=pltpu.VMEM)
    in_hbm = pl.BlockSpec(memory_space=pltpu.HBM)
    operands = [
        pltpu.with_memory_space_constraint(x, pltpu.VMEM if i in kept else pltpu.HBM) if i in kept or i in hbm else x
        for i, x in enumerate(operands)
    ]
    return pl.pallas_call(
        kernel,
        out_shape=outs,
        in_specs=[in_hbm if i in hbm else in_vmem for i in range(len(operands))],
        out_specs=in_hbm if hbm_out else [in_vmem] * len(outs),
        scratch_shapes=scratch,
        input_output_aliases=aliases or {},
        compiler_params=pltpu.CompilerParams(vmem_limit_bytes=VMEM_LIMIT),
        name=name,
    )(*operands)


def local(mesh, signal, jump_sizes, thresholds):
    rows, cols = signal.shape
    chips, cores, halves = mesh.shape["probe"], mesh.shape["sub"], mesh.shape["prof"]
    depth = rows // SUBLANES
    count = float(rows * chips * cores)
    alpha, beta = STEP_LENGTH / (count * count), STEP_LENGTH / count
    offsets = tuple(reversed(range(1, chips)))
    swap = [(0, 1), (1, 0)]
    routes = {
        k: [(z * 2 + c, (z ^ k) * 2 + 1 - c) for z in range(chips) for c in range(2)] for k in offsets
    }

    block = vmem(depth, SUBLANES, cols)
    strip, line, pair = vmem(SUBLANES, cols), vmem(SUBLANES, LANES), vmem(2, cols)
    spread = vmem(depth, SUBLANES, LANES)
    begin_cuts = (0, depth // 8 * 5, depth)
    end_cuts = tuple(depth // 4 * i for i in range(5))

    state, signals, minus, totals, weighted, message, limits, marks = call(
        functools.partial(begin_kernel, chips, count, begin_cuts), "begin",
        [signal, jump_sizes, thresholds.reshape(1, rows)],
        [block, block, strip, strip, strip, pair, line, vmem(chips + 1, cols)], hbm=(0, 1, 2),
        scratch=[
            vmem(1, rows), pltpu.SemaphoreType.DMA((len(begin_cuts) - 1, 2, SUBLANES)), pltpu.SemaphoreType.DMA
        ],
    )
    (const,) = call(functools.partial(suffix_kernel, beta), "suffix", [signals], [block], kept=(0,), aliases={0: 0})
    factor = None
    for iteration in range(ITERS):
        if iteration:
            factor, totals, weighted, message = call(
                sums_kernel, "sums", [own, other, limits, state, minus], [spread, strip, strip, pair], kept=(3, 4)
            )
        sibling = lax.ppermute(message, "sub", swap)
        both = message + sibling
        lower = jnp.where(marks[0:1] > 0.0, message[0:1], sibling[0:1])
        upward = both[0:1]
        downward = both[1:2] + float(rows) * lower + marks[1:2] * upward
        received = [
            lax.ppermute(jnp.where(marks[1 + k : 2 + k] > 0.0, upward, downward), ("probe", "sub"), routes[k])
            for k in offsets
        ]
        scaled = factor is not None
        inner, slope, base = call(
            functools.partial(inner_kernel, alpha, chips, scaled), "inner",
            [state, const, factor if scaled else minus, totals, weighted, message, sibling],
            [block, strip, strip], kept=(0, 1, 2, 3, 4), aliases={0: 0},
        )
        state, own = call(
            functools.partial(outer_kernel, alpha, chips, offsets), "outer", [inner, slope, base, *received],
            [block, line], kept=(0, 1, 2), aliases={0: 0}, scratch=[vmem(len(groups(cols, WIDTH)), depth, SUBLANES, LANES)],
        )
        if halves == 2:
            other = lax.ppermute(own, "prof", swap)
        else:
            own, other = lax.psum(own, "prof"), jnp.zeros_like(own)
    return call(
        functools.partial(end_kernel, end_cuts), "finish", [own, other, limits, state], jax.ShapeDtypeStruct((rows, cols), jnp.float32), kept=(3,),
        hbm_out=True,
        scratch=[spread, block, pltpu.SemaphoreType.DMA((len(end_cuts) - 1, SUBLANES))],
    )


def solution(mesh):
    spec = P(("grp", "probe", "sub"), "prof")
    return jax.shard_map(
        functools.partial(local, mesh),
        mesh=mesh,
        in_specs=(spec, spec, P(("grp", "probe", "sub"))),
        out_specs=spec,
        check_vma=False,
    )
```

```python
import functools

import jax
import jax.numpy as jnp
from jax import lax
from jax.experimental import pallas as pl
from jax.experimental.pallas import tpu as pltpu
from jax.sharding import PartitionSpec as P

ITERS = 8
STEP_LENGTH = 2.0
LANES = 128
SUBLANES = 8
VMEM_LIMIT = 16 * 1024 * 1024
WIDTH, BATCH = 8, 4


def tiles(cols):
    return [slice(j * LANES, (j + 1) * LANES) for j in range(cols // LANES)]


def groups(cols, width):
    cs = tiles(cols)
    return [cs[g : g + width] for g in range(0, len(cs), width)]


def row_weights():
    return (SUBLANES - 1 - lax.broadcasted_iota(jnp.int32, (SUBLANES, LANES), 0)).astype(jnp.float32)


def finish_sums(depth, total, weighted, totals_ref, weighted_ref, message_ref, cols):
    weights = row_weights() * float(depth)
    for j, c in enumerate(tiles(cols)):
        totals_ref[:, c] = total[j]
        weighted_ref[:, c] = weighted[j]
        message_ref[0:1, c] = jnp.sum(total[j], axis=0, keepdims=True)
        message_ref[1:2, c] = jnp.sum(weights * total[j] + weighted[j], axis=0, keepdims=True)


def begin_kernel(chips, count, cuts, signal_hbm, jumps_hbm, thresholds_hbm, state_ref, signal_ref, minus_ref, totals_ref,
                 weighted_ref, message_ref, limits_ref, marks_ref, thresholds_ref, sems, limits_sem):
    depth, _, cols = state_ref.shape
    rows = depth * SUBLANES

    def copies(part):
        low, high = cuts[part], cuts[part + 1]
        for a, (src, dst) in enumerate(((jumps_hbm, state_ref), (signal_hbm, signal_ref))):
            for s in range(SUBLANES):
                yield pltpu.make_async_copy(
                    src.at[pl.ds(s * depth + low, high - low), :], dst.at[pl.ds(low, high - low), s, :],
                    sems.at[part, a, s],
                )

    limits_copy = pltpu.make_async_copy(thresholds_hbm, thresholds_ref, limits_sem)
    limits_copy.start()
    for part in range(len(cuts) - 1):
        for copy in copies(part):
            copy.start()

    chip, core = lax.axis_index("probe"), lax.axis_index("sub")
    later = (chips - 1 - chip).astype(jnp.float32) * (2.0 * rows)
    marks = [(core == 0).astype(jnp.float32), later, jnp.float32(rows)]
    marks += [(jnp.bitwise_xor(chip, k) > chip).astype(jnp.float32) for k in range(1, chips)]
    for i, mark in enumerate(marks):
        marks_ref[i : i + 1, :] = jnp.full((1, cols), mark, jnp.float32)

    limits_copy.wait()
    sublane = lax.broadcasted_iota(jnp.int32, (SUBLANES, LANES), 0)
    lane = lax.broadcasted_iota(jnp.int32, (SUBLANES, LANES), 1)
    limits = jnp.zeros((SUBLANES, LANES), jnp.float32)
    for s in range(SUBLANES):
        tile, offset = divmod(s * depth, LANES)
        line = jnp.broadcast_to(thresholds_ref[0:1, tile * LANES : (tile + 1) * LANES], (SUBLANES, LANES))
        for copy in range(LANES // depth):
            shift = (copy * depth - offset) % LANES
            moved = pltpu.roll(line, shift, 1) if shift else line
            limits = jnp.where((sublane == s) & (lane // depth == copy), moved, limits)
    limits_ref[...] = limits

    zero = jnp.zeros((SUBLANES, LANES), jnp.float32)
    grouped = groups(cols, WIDTH)
    carries = [([zero] * len(group), [zero] * len(group), [zero] * len(group)) for group in grouped]
    for part in range(len(cuts) - 1):
        for copy in copies(part):
            copy.wait()
        for g, group in enumerate(grouped):

            def step(i, carry, group=group, low=cuts[part]):
                total, weighted, signals = (list(x) for x in carry)
                for q in range(BATCH):
                    k = low + i * BATCH + q
                    for j, c in enumerate(group):
                        total[j] = total[j] + state_ref[k, :, c]
                        weighted[j] = weighted[j] + total[j]
                        signals[j] = signals[j] + signal_ref[k, :, c]
                return total, weighted, signals

            carries[g] = lax.fori_loop(0, (cuts[part + 1] - cuts[part]) // BATCH, step, carries[g])
    total, weighted = [], []
    for group, carry in zip(grouped, carries):
        for c, t, w, x in zip(group, *carry):
            minus = x * -count
            minus_ref[:, c] = minus
            total.append(t)
            weighted.append(w + minus)
    finish_sums(depth, total, weighted, totals_ref, weighted_ref, message_ref, cols)


def suffix_kernel(beta, signal_ref, const_ref):
    depth, _, cols = signal_ref.shape
    zero = jnp.zeros((SUBLANES, LANES), jnp.float32)
    for group in groups(cols, WIDTH):

        def step(i, suffix, group=group):
            suffix = list(suffix)
            start = depth - (i + 1) * BATCH
            results = []
            for k in reversed([start + q for q in range(BATCH)]):
                for j, c in enumerate(group):
                    suffix[j] = suffix[j] + signal_ref[k, :, c]
                    results.append((k, c, suffix[j] * beta))
            for k, c, value in results:
                const_ref[k, :, c] = value
            return suffix

        lax.fori_loop(0, depth // BATCH, step, [zero] * len(group))


def shrink(own_ref, other_ref, limits_ref, factor_ref):
    squares = own_ref[...] + other_ref[...]
    factor = jnp.maximum(0.0, 1.0 - limits_ref[...] / jnp.sqrt(squares + 1e-06))
    for k in range(factor_ref.shape[0]):
        factor_ref[k] = jnp.broadcast_to(factor[:, k : k + 1], (SUBLANES, LANES))


def sums_kernel(own_ref, other_ref, limits_ref, state_ref, minus_ref, factor_ref, totals_ref, weighted_ref, message_ref):
    depth, _, cols = state_ref.shape
    shrink(own_ref, other_ref, limits_ref, factor_ref)
    zero = jnp.zeros((SUBLANES, LANES), jnp.float32)
    totals, weights = [], []
    for group in groups(cols, WIDTH):
        total, weighted = [zero] * len(group), [minus_ref[:, c] for c in group]
        for k in range(depth):
            factor = factor_ref[k]
            for j, c in enumerate(group):
                total[j] = total[j] + state_ref[k, :, c] * factor
                weighted[j] = weighted[j] + total[j]
        totals += total
        weights += weighted
    finish_sums(depth, totals, weights, totals_ref, weighted_ref, message_ref, cols)


def route_kernel(offsets, message_ref, sibling_ref, marks_ref, *out_refs):
    for c in tiles(message_ref.shape[1]):
        own, sibling = message_ref[0:1, c], sibling_ref[0:1, c]
        lower = jnp.where(marks_ref[0:1, c] > 0.0, own, sibling)
        upward = own + sibling
        weighted = message_ref[1:2, c] + sibling_ref[1:2, c]
        downward = weighted + marks_ref[1:2, c] * upward + marks_ref[2:3, c] * lower
        for k, ref in zip(offsets, out_refs):
            ref[:, c] = jnp.where(marks_ref[2 + k : 3 + k, c] > 0.0, upward, downward)


def prefix_rows(x, sublane):
    for shift in (1, 2, 4):
        x = x + jnp.where(sublane >= shift, pltpu.roll(x, shift, 0), 0.0)
    return x


def suffix_rows(x, sublane):
    for shift in (1, 2, 4):
        x = x + jnp.where(sublane < SUBLANES - shift, pltpu.roll(x, SUBLANES - shift, 0), 0.0)
    return x


def inner_kernel(alpha, chips, scaled, state_ref, const_ref, factor_ref, totals_ref, weighted_ref, message_ref,
                 sibling_ref, inner_ref, slope_ref, base_ref):
    depth, _, cols = state_ref.shape
    rows = float(depth * SUBLANES)
    cs = tiles(cols)
    chip, core = lax.axis_index("probe"), lax.axis_index("sub")
    first = (core == 0).astype(jnp.float32)
    later = (chips - 1 - chip).astype(jnp.float32) * (2.0 * rows)
    sublane = lax.broadcasted_iota(jnp.int32, (SUBLANES, LANES), 0)
    weights = row_weights() * float(depth)

    zero = jnp.zeros((SUBLANES, LANES), jnp.float32)
    for group in groups(cols, WIDTH):

        def step(i, carry, group=group):
            running, double = (list(x) for x in carry)
            start = depth - (i + 1) * BATCH
            results = []
            for k in reversed([start + q for q in range(BATCH)]):
                factor = factor_ref[k] if scaled else None
                for j, c in enumerate(group):
                    jump = state_ref[k, :, c]
                    if scaled:
                        jump = jump * factor
                    double[j] = double[j] + running[j]
                    results.append((k, c, jump + const_ref[k, :, c] - double[j]))
                    running[j] = running[j] - jump * alpha
            for k, c, value in results:
                inner_ref[k, :, c] = value
            return running, double

        lax.fori_loop(
            0, depth // BATCH, step, ([totals_ref[:, c] * alpha for c in group], [zero] * len(group))
        )

    for c in cs:
        total = totals_ref[:, c]
        before = jnp.where(sublane >= 1, pltpu.roll(prefix_rows(total, sublane), 1, 0), 0.0)
        chunk = before * float(depth) + weighted_ref[:, c]
        after = jnp.where(
            sublane < SUBLANES - 1, pltpu.roll(suffix_rows(chunk, sublane), SUBLANES - 1, 0), 0.0
        )
        own, sibling = message_ref[0:1, c], sibling_ref[0:1, c]
        lower = first * own + (1.0 - first) * sibling
        shift = (1.0 - first) * lower
        base = later * (own + sibling) + first * (rows * lower + sibling_ref[1:2, c])
        slope_ref[:, c] = alpha * (before + shift)
        base_ref[:, c] = alpha * (after + base + weights * shift)


def outer_kernel(alpha, chips, offsets, inner_ref, slope_ref, base_ref, *refs):
    received, (state_ref, squares_ref, wide_ref) = refs[: len(offsets)], refs[len(offsets) :]
    depth, _, cols = inner_ref.shape
    rows = float(depth * SUBLANES)
    chip, core = lax.axis_index("probe"), lax.axis_index("sub")
    later = (chips - 1 - chip).astype(jnp.float32) * (2.0 * rows) + (core == 0).astype(jnp.float32) * rows
    weights = row_weights() * float(depth) + later
    earlier = [(jnp.bitwise_xor(chip, k) < chip).astype(jnp.float32) for k in offsets]

    grouped = groups(cols, WIDTH)
    for g, group in enumerate(grouped):
        slope, value = [], []
        for c in group:
            above = sum(e * ref[:, c] for e, ref in zip(earlier, received))
            below = sum((1.0 - e) * ref[:, c] for e, ref in zip(earlier, received))
            above, below = above * alpha, below * alpha
            slope.append(slope_ref[:, c] + above)
            value.append(base_ref[:, c] + below + weights * above + slope[-1])

        def step(i, value, g=g, group=group, slope=slope):
            value = list(value)
            start = depth - (i + 1) * BATCH
            results, sums = [], []
            for k in reversed([start + q for q in range(BATCH)]):
                squares = []
                for j, c in enumerate(group):
                    stepped = inner_ref[k, :, c] - value[j]
                    value[j] = value[j] + slope[j]
                    results.append((k, c, stepped))
                    squares.append(stepped * stepped)
                while len(squares) > 1:
                    squares = [a + b for a, b in zip(squares[::2], squares[1::2])]
                sums.append((k, squares[0]))
            for k, c, stepped in results:
                state_ref[k, :, c] = stepped
            for k, total in sums:
                wide_ref[g, k] = total
            return value

        lax.fori_loop(0, depth // BATCH, step, value, unroll=4)
    lane = lax.broadcasted_iota(jnp.int32, (SUBLANES, LANES), 1)
    parts = []
    for low in range(0, depth, SUBLANES):
        part = jnp.zeros((SUBLANES, LANES), jnp.float32)
        for k in range(low, low + SUBLANES):
            total = jnp.sum(sum(wide_ref[g, k] for g in range(len(grouped))), axis=1, keepdims=True)
            part = jnp.where(lane % depth == k, jnp.broadcast_to(total, part.shape), part)
        parts.append(part)
    squares_ref[...] = sum(parts)


def end_kernel(cuts, own_ref, other_ref, limits_ref, state_ref, out_hbm, factor_ref, jumps_ref, sems):
    depth, _, cols = state_ref.shape
    shrink(own_ref, other_ref, limits_ref, factor_ref)
    copies = []
    for part in range(len(cuts) - 1):
        low, high = cuts[part], cuts[part + 1]
        for group in groups(cols, WIDTH):

            def step(i, carry, low=low, group=group):
                results = []
                for q in range(BATCH):
                    k = low + i * BATCH + q
                    factor = factor_ref[k]
                    results += [(k, c, state_ref[k, :, c] * factor) for c in group]
                for k, c, value in results:
                    jumps_ref[k, :, c] = value
                return carry

            lax.fori_loop(0, (high - low) // BATCH, step, 0)
        for s in range(SUBLANES):
            copy = pltpu.make_async_copy(
                jumps_ref.at[pl.ds(low, high - low), s, :], out_hbm.at[pl.ds(s * depth + low, high - low), :],
                sems.at[part, s],
            )
            copy.start()
            copies.append(copy)
    for copy in copies:
        copy.wait()


def vmem(*shape):
    return pltpu.VMEM(shape, jnp.float32)


def call(kernel, name, operands, outs, kept=(), scratch=(), aliases=None, hbm=(), hbm_out=False):
    in_vmem = pl.BlockSpec(memory_space=pltpu.VMEM)
    in_hbm = pl.BlockSpec(memory_space=pltpu.HBM)
    operands = [
        pltpu.with_memory_space_constraint(x, pltpu.VMEM if i in kept else pltpu.HBM) if i in kept or i in hbm else x
        for i, x in enumerate(operands)
    ]
    return pl.pallas_call(
        kernel,
        out_shape=outs,
        in_specs=[in_hbm if i in hbm else in_vmem for i in range(len(operands))],
        out_specs=in_hbm if hbm_out else [in_vmem] * len(outs),
        scratch_shapes=scratch,
        input_output_aliases=aliases or {},
        compiler_params=pltpu.CompilerParams(vmem_limit_bytes=VMEM_LIMIT),
        name=name,
    )(*operands)


def local(mesh, signal, jump_sizes, thresholds):
    rows, cols = signal.shape
    chips, cores, halves = mesh.shape["probe"], mesh.shape["sub"], mesh.shape["prof"]
    depth = rows // SUBLANES
    count = float(rows * chips * cores)
    alpha, beta = STEP_LENGTH / (count * count), STEP_LENGTH / count
    offsets = tuple(reversed(range(1, chips)))
    swap = [(0, 1), (1, 0)]
    routes = {
        k: [(z * 2 + c, (z ^ k) * 2 + 1 - c) for z in range(chips) for c in range(2)] for k in offsets
    }

    block = vmem(depth, SUBLANES, cols)
    strip, line, pair = vmem(SUBLANES, cols), vmem(SUBLANES, LANES), vmem(2, cols)
    spread = vmem(depth, SUBLANES, LANES)
    begin_cuts = (0, depth // 8 * 5, depth)
    end_cuts = tuple(depth // 8 * i for i in (0, 1, 3, 5, 8))

    state, signals, minus, totals, weighted, message, limits, marks = call(
        functools.partial(begin_kernel, chips, count, begin_cuts), "begin",
        [signal, jump_sizes, thresholds.reshape(1, rows)],
        [block, block, strip, strip, strip, pair, line, vmem(chips + 2, cols)], hbm=(0, 1, 2),
        scratch=[
            vmem(1, rows), pltpu.SemaphoreType.DMA((len(begin_cuts) - 1, 2, SUBLANES)), pltpu.SemaphoreType.DMA
        ],
    )
    (const,) = call(functools.partial(suffix_kernel, beta), "suffix", [signals], [block], kept=(0,), aliases={0: 0})
    factor = None
    for iteration in range(ITERS):
        if iteration:
            factor, totals, weighted, message = call(
                sums_kernel, "sums", [own, other, limits, state, minus], [spread, strip, strip, pair], kept=(3, 4)
            )
        sibling = lax.ppermute(message, "sub", swap)
        routed = call(
            functools.partial(route_kernel, offsets), "route", [message, sibling, marks], [vmem(1, cols)] * len(offsets)
        )
        received = [lax.ppermute(x, ("probe", "sub"), routes[k]) for k, x in zip(offsets, routed)]
        scaled = factor is not None
        inner, slope, base = call(
            functools.partial(inner_kernel, alpha, chips, scaled), "inner",
            [state, const, factor if scaled else minus, totals, weighted, message, sibling],
            [block, strip, strip], kept=(0, 1, 2, 3, 4), aliases={0: 0},
        )
        state, own = call(
            functools.partial(outer_kernel, alpha, chips, offsets), "outer", [inner, slope, base, *received],
            [block, line], kept=(0, 1, 2), aliases={0: 0}, scratch=[vmem(len(groups(cols, WIDTH)), depth, SUBLANES, LANES)],
        )
        if halves == 2:
            other = lax.ppermute(own, "prof", swap)
        else:
            own, other = lax.psum(own, "prof"), jnp.zeros_like(own)
    return call(
        functools.partial(end_kernel, end_cuts), "finish", [own, other, limits, state], jax.ShapeDtypeStruct((rows, cols), jnp.float32), kept=(3,),
        hbm_out=True,
        scratch=[spread, block, pltpu.SemaphoreType.DMA((len(end_cuts) - 1, SUBLANES))],
    )


def solution(mesh):
    spec = P(("grp", "probe", "sub"), "prof")
    return jax.shard_map(
        functools.partial(local, mesh),
        mesh=mesh,
        in_specs=(spec, spec, P(("grp", "probe", "sub"))),
        out_specs=spec,
        check_vma=False,
    )
```

```python
import functools

import jax
import jax.numpy as jnp
from jax import lax
from jax.experimental import pallas as pl
from jax.experimental.pallas import tpu as pltpu
from jax.sharding import PartitionSpec as P

ITERS = 8
STEP_LENGTH = 2.0
LANES = 128
SUBLANES = 8
VMEM_LIMIT = 16 * 1024 * 1024
WIDTH, BATCH = 8, 4


def tiles(cols):
    return [slice(j * LANES, (j + 1) * LANES) for j in range(cols // LANES)]


def groups(cols, width):
    cs = tiles(cols)
    return [cs[g : g + width] for g in range(0, len(cs), width)]


def row_weights():
    return (SUBLANES - 1 - lax.broadcasted_iota(jnp.int32, (SUBLANES, LANES), 0)).astype(jnp.float32)


def finish_sums(depth, total, weighted, totals_ref, weighted_ref, message_ref, cols):
    weights = row_weights() * float(depth)
    for j, c in enumerate(tiles(cols)):
        totals_ref[:, c] = total[j]
        weighted_ref[:, c] = weighted[j]
        message_ref[0:1, c] = jnp.sum(total[j], axis=0, keepdims=True)
        message_ref[1:2, c] = jnp.sum(weights * total[j] + weighted[j], axis=0, keepdims=True)


def begin_kernel(chips, count, cuts, signal_hbm, jumps_hbm, thresholds_hbm, state_ref, signal_ref, minus_ref, totals_ref,
                 weighted_ref, message_ref, limits_ref, marks_ref, thresholds_ref, sems, limits_sem):
    depth, _, cols = state_ref.shape
    rows = depth * SUBLANES

    def copies(part):
        low, high = cuts[part], cuts[part + 1]
        for a, (src, dst) in enumerate(((jumps_hbm, state_ref), (signal_hbm, signal_ref))):
            for s in range(SUBLANES):
                yield pltpu.make_async_copy(
                    src.at[pl.ds(s * depth + low, high - low), :], dst.at[pl.ds(low, high - low), s, :],
                    sems.at[part, a, s],
                )

    limits_copy = pltpu.make_async_copy(thresholds_hbm, thresholds_ref, limits_sem)
    limits_copy.start()
    for part in range(len(cuts) - 1):
        for copy in copies(part):
            copy.start()

    chip, core = lax.axis_index("probe"), lax.axis_index("sub")
    later = (chips - 1 - chip).astype(jnp.float32) * (2.0 * rows)
    marks = [(core == 0).astype(jnp.float32), later, jnp.float32(rows)]
    marks += [(jnp.bitwise_xor(chip, k) > chip).astype(jnp.float32) for k in range(1, chips)]
    for i, mark in enumerate(marks):
        marks_ref[i : i + 1, :] = jnp.full((1, cols), mark, jnp.float32)

    limits_copy.wait()
    sublane = lax.broadcasted_iota(jnp.int32, (SUBLANES, LANES), 0)
    lane = lax.broadcasted_iota(jnp.int32, (SUBLANES, LANES), 1)
    limits = jnp.zeros((SUBLANES, LANES), jnp.float32)
    for s in range(SUBLANES):
        tile, offset = divmod(s * depth, LANES)
        line = jnp.broadcast_to(thresholds_ref[0:1, tile * LANES : (tile + 1) * LANES], (SUBLANES, LANES))
        for copy in range(LANES // depth):
            shift = (copy * depth - offset) % LANES
            moved = pltpu.roll(line, shift, 1) if shift else line
            limits = jnp.where((sublane == s) & (lane // depth == copy), moved, limits)
    limits_ref[...] = limits

    zero = jnp.zeros((SUBLANES, LANES), jnp.float32)
    grouped = groups(cols, WIDTH)
    carries = [([zero] * len(group), [zero] * len(group), [zero] * len(group)) for group in grouped]
    for part in range(len(cuts) - 1):
        for copy in copies(part):
            copy.wait()
        for g, group in enumerate(grouped):

            def step(i, carry, group=group, low=cuts[part]):
                total, weighted, signals = (list(x) for x in carry)
                for q in range(BATCH):
                    k = low + i * BATCH + q
                    for j, c in enumerate(group):
                        total[j] = total[j] + state_ref[k, :, c]
                        weighted[j] = weighted[j] + total[j]
                        signals[j] = signals[j] + signal_ref[k, :, c]
                return total, weighted, signals

            carries[g] = lax.fori_loop(0, (cuts[part + 1] - cuts[part]) // BATCH, step, carries[g])
    total, weighted = [], []
    for group, carry in zip(grouped, carries):
        for c, t, w, x in zip(group, *carry):
            minus = x * -count
            minus_ref[:, c] = minus
            total.append(t)
            weighted.append(w + minus)
    finish_sums(depth, total, weighted, totals_ref, weighted_ref, message_ref, cols)


def suffix_kernel(beta, signal_ref, const_ref):
    depth, _, cols = signal_ref.shape
    zero = jnp.zeros((SUBLANES, LANES), jnp.float32)
    for group in groups(cols, WIDTH):

        def step(i, suffix, group=group):
            suffix = list(suffix)
            start = depth - (i + 1) * BATCH
            results = []
            for k in reversed([start + q for q in range(BATCH)]):
                for j, c in enumerate(group):
                    suffix[j] = suffix[j] + signal_ref[k, :, c]
                    results.append((k, c, suffix[j] * beta))
            for k, c, value in results:
                const_ref[k, :, c] = value
            return suffix

        lax.fori_loop(0, depth // BATCH, step, [zero] * len(group))


def shrink(own_ref, other_ref, limits_ref, factor_ref):
    squares = own_ref[...] + other_ref[...]
    factor = jnp.maximum(0.0, 1.0 - limits_ref[...] / jnp.sqrt(squares + 1e-06))
    for k in range(factor_ref.shape[0]):
        factor_ref[k] = jnp.broadcast_to(factor[:, k : k + 1], (SUBLANES, LANES))


def sums_kernel(own_ref, other_ref, limits_ref, state_ref, minus_ref, factor_ref, totals_ref, weighted_ref, message_ref):
    depth, _, cols = state_ref.shape
    shrink(own_ref, other_ref, limits_ref, factor_ref)
    zero = jnp.zeros((SUBLANES, LANES), jnp.float32)
    totals, weights = [], []
    for group in groups(cols, WIDTH):
        total, weighted = [zero] * len(group), [minus_ref[:, c] for c in group]
        for k in range(depth):
            factor = factor_ref[k]
            for j, c in enumerate(group):
                total[j] = total[j] + state_ref[k, :, c] * factor
                weighted[j] = weighted[j] + total[j]
        totals += total
        weights += weighted
    finish_sums(depth, totals, weights, totals_ref, weighted_ref, message_ref, cols)


def route_kernel(offsets, message_ref, sibling_ref, marks_ref, *out_refs):
    for c in tiles(message_ref.shape[1]):
        own, sibling = message_ref[0:1, c], sibling_ref[0:1, c]
        lower = jnp.where(marks_ref[0:1, c] > 0.0, own, sibling)
        upward = own + sibling
        weighted = message_ref[1:2, c] + sibling_ref[1:2, c]
        downward = weighted + marks_ref[1:2, c] * upward + marks_ref[2:3, c] * lower
        for k, ref in zip(offsets, out_refs):
            ref[:, c] = jnp.where(marks_ref[2 + k : 3 + k, c] > 0.0, upward, downward)


def prefix_rows(x, sublane):
    for shift in (1, 2, 4):
        x = x + jnp.where(sublane >= shift, pltpu.roll(x, shift, 0), 0.0)
    return x


def suffix_rows(x, sublane):
    for shift in (1, 2, 4):
        x = x + jnp.where(sublane < SUBLANES - shift, pltpu.roll(x, SUBLANES - shift, 0), 0.0)
    return x


def inner_kernel(alpha, chips, scaled, state_ref, const_ref, factor_ref, totals_ref, weighted_ref, message_ref,
                 sibling_ref, inner_ref, slope_ref, base_ref):
    depth, _, cols = state_ref.shape
    rows = float(depth * SUBLANES)
    cs = tiles(cols)
    chip, core = lax.axis_index("probe"), lax.axis_index("sub")
    first = (core == 0).astype(jnp.float32)
    later = (chips - 1 - chip).astype(jnp.float32) * (2.0 * rows)
    sublane = lax.broadcasted_iota(jnp.int32, (SUBLANES, LANES), 0)
    weights = row_weights() * float(depth)

    zero = jnp.zeros((SUBLANES, LANES), jnp.float32)
    for group in groups(cols, WIDTH):
        running, double = [totals_ref[:, c] * alpha for c in group], [zero] * len(group)
        for start in reversed(range(0, depth, BATCH)):
            results = []
            for k in reversed(range(start, start + BATCH)):
                factor = factor_ref[k] if scaled else None
                for j, c in enumerate(group):
                    jump = inner_ref[k, :, c]
                    if scaled:
                        jump = jump * factor
                    double[j] = double[j] + running[j]
                    results.append((k, c, jump + const_ref[k, :, c] - double[j]))
                    running[j] = running[j] - jump * alpha
            for k, c, value in results:
                inner_ref[k, :, c] = value

    for c in cs:
        total = totals_ref[:, c]
        before = jnp.where(sublane >= 1, pltpu.roll(prefix_rows(total, sublane), 1, 0), 0.0)
        chunk = before * float(depth) + weighted_ref[:, c]
        after = jnp.where(
            sublane < SUBLANES - 1, pltpu.roll(suffix_rows(chunk, sublane), SUBLANES - 1, 0), 0.0
        )
        own, sibling = message_ref[0:1, c], sibling_ref[0:1, c]
        lower = first * own + (1.0 - first) * sibling
        shift = (1.0 - first) * lower
        base = later * (own + sibling) + first * (rows * lower + sibling_ref[1:2, c])
        slope_ref[:, c] = alpha * (before + shift)
        base_ref[:, c] = alpha * (after + base + weights * shift)


def outer_kernel(alpha, chips, offsets, inner_ref, slope_ref, base_ref, *refs):
    received, (state_ref, squares_ref) = refs[: len(offsets)], refs[len(offsets) :]
    depth, _, cols = inner_ref.shape
    rows = float(depth * SUBLANES)
    chip, core = lax.axis_index("probe"), lax.axis_index("sub")
    later = (chips - 1 - chip).astype(jnp.float32) * (2.0 * rows) + (core == 0).astype(jnp.float32) * rows
    weights = row_weights() * float(depth) + later
    earlier = [(jnp.bitwise_xor(chip, k) < chip).astype(jnp.float32) for k in offsets]

    lane = lax.broadcasted_iota(jnp.int32, (SUBLANES, LANES), 1) % depth
    sums = [jnp.zeros((SUBLANES, LANES), jnp.float32)] * 4
    for group in groups(cols, WIDTH):
        slope, value = [], []
        for c in group:
            above = sum(e * ref[:, c] for e, ref in zip(earlier, received))
            below = sum((1.0 - e) * ref[:, c] for e, ref in zip(earlier, received))
            above, below = above * alpha, below * alpha
            slope.append(slope_ref[:, c] + above)
            value.append(base_ref[:, c] + below + weights * above + slope[-1])

        for k in reversed(range(depth)):
            squares = []
            for j, c in enumerate(group):
                stepped = state_ref[k, :, c] - value[j]
                value[j] = value[j] + slope[j]
                state_ref[k, :, c] = stepped
                squares.append(stepped * stepped)
            while len(squares) > 1:
                squares = [a + b for a, b in zip(squares[::2], squares[1::2])]
            total = jnp.broadcast_to(jnp.sum(squares[0], axis=1, keepdims=True), (SUBLANES, LANES))
            sums[k % 4] = sums[k % 4] + jnp.where(lane == k, total, 0.0)
    squares_ref[...] = (sums[0] + sums[1]) + (sums[2] + sums[3])


def end_kernel(cuts, own_ref, other_ref, limits_ref, state_ref, out_hbm, factor_ref, jumps_ref, sems):
    depth, _, cols = state_ref.shape
    shrink(own_ref, other_ref, limits_ref, factor_ref)
    copies = []
    for part in range(len(cuts) - 1):
        low, high = cuts[part], cuts[part + 1]
        for group in groups(cols, WIDTH):

            def step(i, carry, low=low, group=group):
                results = []
                for q in range(BATCH):
                    k = low + i * BATCH + q
                    factor = factor_ref[k]
                    results += [(k, c, state_ref[k, :, c] * factor) for c in group]
                for k, c, value in results:
                    jumps_ref[k, :, c] = value
                return carry

            lax.fori_loop(0, (high - low) // BATCH, step, 0)
        for s in range(SUBLANES):
            copy = pltpu.make_async_copy(
                jumps_ref.at[pl.ds(low, high - low), s, :], out_hbm.at[pl.ds(s * depth + low, high - low), :],
                sems.at[part, s],
            )
            copy.start()
            copies.append(copy)
    for copy in copies:
        copy.wait()


def vmem(*shape):
    return pltpu.VMEM(shape, jnp.float32)


def call(kernel, name, operands, outs, kept=(), scratch=(), aliases=None, hbm=(), hbm_out=False):
    in_vmem = pl.BlockSpec(memory_space=pltpu.VMEM)
    in_hbm = pl.BlockSpec(memory_space=pltpu.HBM)
    operands = [
        pltpu.with_memory_space_constraint(x, pltpu.VMEM if i in kept else pltpu.HBM) if i in kept or i in hbm else x
        for i, x in enumerate(operands)
    ]
    return pl.pallas_call(
        kernel,
        out_shape=outs,
        in_specs=[in_hbm if i in hbm else in_vmem for i in range(len(operands))],
        out_specs=in_hbm if hbm_out else [in_vmem] * len(outs),
        scratch_shapes=scratch,
        input_output_aliases=aliases or {},
        compiler_params=pltpu.CompilerParams(vmem_limit_bytes=VMEM_LIMIT),
        name=name,
    )(*operands)


def local(mesh, signal, jump_sizes, thresholds):
    rows, cols = signal.shape
    chips, cores, halves = mesh.shape["probe"], mesh.shape["sub"], mesh.shape["prof"]
    depth = rows // SUBLANES
    count = float(rows * chips * cores)
    alpha, beta = STEP_LENGTH / (count * count), STEP_LENGTH / count
    offsets = tuple(reversed(range(1, chips)))
    swap = [(0, 1), (1, 0)]
    routes = {
        k: [(z * 2 + c, (z ^ k) * 2 + 1 - c) for z in range(chips) for c in range(2)] for k in offsets
    }

    block = vmem(depth, SUBLANES, cols)
    strip, line, pair = vmem(SUBLANES, cols), vmem(SUBLANES, LANES), vmem(2, cols)
    spread = vmem(depth, SUBLANES, LANES)
    begin_cuts = (0, depth // 8 * 5, depth)
    end_cuts = tuple(depth // 8 * i for i in (0, 1, 3, 5, 8))

    state, signals, minus, totals, weighted, message, limits, marks = call(
        functools.partial(begin_kernel, chips, count, begin_cuts), "begin",
        [signal, jump_sizes, thresholds.reshape(1, rows)],
        [block, block, strip, strip, strip, pair, line, vmem(chips + 2, cols)], hbm=(0, 1, 2),
        scratch=[
            vmem(1, rows), pltpu.SemaphoreType.DMA((len(begin_cuts) - 1, 2, SUBLANES)), pltpu.SemaphoreType.DMA
        ],
    )
    (const,) = call(functools.partial(suffix_kernel, beta), "suffix", [signals], [block], kept=(0,), aliases={0: 0})
    factor = None
    for iteration in range(ITERS):
        if iteration:
            factor, totals, weighted, message = call(
                sums_kernel, "sums", [own, other, limits, state, minus], [spread, strip, strip, pair], kept=(3, 4)
            )
        sibling = lax.ppermute(message, "sub", swap)
        routed = call(
            functools.partial(route_kernel, offsets), "route", [message, sibling, marks], [vmem(1, cols)] * len(offsets)
        )
        received = [lax.ppermute(x, ("probe", "sub"), routes[k]) for k, x in zip(offsets, routed)]
        scaled = factor is not None
        inner, slope, base = call(
            functools.partial(inner_kernel, alpha, chips, scaled), "inner",
            [state, const, factor if scaled else minus, totals, weighted, message, sibling],
            [block, strip, strip], kept=(0, 1, 2, 3, 4), aliases={0: 0},
        )
        state, own = call(
            functools.partial(outer_kernel, alpha, chips, offsets), "outer", [inner, slope, base, *received],
            [block, line], kept=(0, 1, 2), aliases={0: 0},
        )
        if halves == 2:
            other = lax.ppermute(own, "prof", swap)
        else:
            own, other = lax.psum(own, "prof"), jnp.zeros_like(own)
    return call(
        functools.partial(end_kernel, end_cuts), "finish", [own, other, limits, state], jax.ShapeDtypeStruct((rows, cols), jnp.float32), kept=(3,),
        hbm_out=True,
        scratch=[spread, block, pltpu.SemaphoreType.DMA((len(end_cuts) - 1, SUBLANES))],
    )


def solution(mesh):
    spec = P(("grp", "probe", "sub"), "prof")
    return jax.shard_map(
        functools.partial(local, mesh),
        mesh=mesh,
        in_specs=(spec, spec, P(("grp", "probe", "sub"))),
        out_specs=spec,
        check_vma=False,
    )
```

```python
import functools

import jax
import jax.numpy as jnp
from jax import lax
from jax.experimental import pallas as pl
from jax.experimental.pallas import tpu as pltpu
from jax.sharding import PartitionSpec as P

ITERS = 8
STEP_LENGTH = 2.0
LANES = 128
SUBLANES = 8
VMEM_LIMIT = 16 * 1024 * 1024
WIDTH, BATCH = 8, 4


def tiles(cols):
    return [slice(j * LANES, (j + 1) * LANES) for j in range(cols // LANES)]


def groups(cols, width):
    cs = tiles(cols)
    return [cs[g : g + width] for g in range(0, len(cs), width)]


def row_weights():
    return (SUBLANES - 1 - lax.broadcasted_iota(jnp.int32, (SUBLANES, LANES), 0)).astype(jnp.float32)


def finish_sums(depth, total, weighted, totals_ref, weighted_ref, message_ref, cols):
    weights = row_weights() * float(depth)
    for j, c in enumerate(tiles(cols)):
        totals_ref[:, c] = total[j]
        weighted_ref[:, c] = weighted[j]
        message_ref[0:1, c] = jnp.sum(total[j], axis=0, keepdims=True)
        message_ref[1:2, c] = jnp.sum(weights * total[j] + weighted[j], axis=0, keepdims=True)


def begin_kernel(chips, count, cuts, signal_hbm, jumps_hbm, thresholds_hbm, state_ref, signal_ref, minus_ref, totals_ref,
                 weighted_ref, message_ref, limits_ref, marks_ref, thresholds_ref, sems, limits_sem):
    depth, _, cols = state_ref.shape
    rows = depth * SUBLANES

    def copies(part):
        low, high = cuts[part], cuts[part + 1]
        for a, (src, dst) in enumerate(((jumps_hbm, state_ref), (signal_hbm, signal_ref))):
            for s in range(SUBLANES):
                yield pltpu.make_async_copy(
                    src.at[pl.ds(s * depth + low, high - low), :], dst.at[pl.ds(low, high - low), s, :],
                    sems.at[part, a, s],
                )

    limits_copy = pltpu.make_async_copy(thresholds_hbm, thresholds_ref, limits_sem)
    limits_copy.start()
    for part in range(len(cuts) - 1):
        for copy in copies(part):
            copy.start()

    chip, core = lax.axis_index("probe"), lax.axis_index("sub")
    later = (chips - 1 - chip).astype(jnp.float32) * (2.0 * rows)
    marks = [(core == 0).astype(jnp.float32), later, jnp.float32(rows)]
    marks += [(jnp.bitwise_xor(chip, k) > chip).astype(jnp.float32) for k in range(1, chips)]
    for i, mark in enumerate(marks):
        marks_ref[i : i + 1, :] = jnp.full((1, cols), mark, jnp.float32)

    limits_copy.wait()
    sublane = lax.broadcasted_iota(jnp.int32, (SUBLANES, LANES), 0)
    lane = lax.broadcasted_iota(jnp.int32, (SUBLANES, LANES), 1)
    limits = jnp.zeros((SUBLANES, LANES), jnp.float32)
    for s in range(SUBLANES):
        tile, offset = divmod(s * depth, LANES)
        line = jnp.broadcast_to(thresholds_ref[0:1, tile * LANES : (tile + 1) * LANES], (SUBLANES, LANES))
        for copy in range(LANES // depth):
            shift = (copy * depth - offset) % LANES
            moved = pltpu.roll(line, shift, 1) if shift else line
            limits = jnp.where((sublane == s) & (lane // depth == copy), moved, limits)
    limits_ref[...] = limits

    zero = jnp.zeros((SUBLANES, LANES), jnp.float32)
    grouped = groups(cols, WIDTH)
    carries = [([zero] * len(group), [zero] * len(group), [zero] * len(group)) for group in grouped]
    for part in range(len(cuts) - 1):
        for copy in copies(part):
            copy.wait()
        for g, group in enumerate(grouped):

            def step(i, carry, group=group, low=cuts[part]):
                total, weighted, signals = (list(x) for x in carry)
                for q in range(BATCH):
                    k = low + i * BATCH + q
                    for j, c in enumerate(group):
                        total[j] = total[j] + state_ref[k, :, c]
                        weighted[j] = weighted[j] + total[j]
                        signals[j] = signals[j] + signal_ref[k, :, c]
                return total, weighted, signals

            carries[g] = lax.fori_loop(0, (cuts[part + 1] - cuts[part]) // BATCH, step, carries[g])
    total, weighted = [], []
    for group, carry in zip(grouped, carries):
        for c, t, w, x in zip(group, *carry):
            minus = x * -count
            minus_ref[:, c] = minus
            total.append(t)
            weighted.append(w + minus)
    finish_sums(depth, total, weighted, totals_ref, weighted_ref, message_ref, cols)


def suffix_kernel(beta, signal_ref, const_ref):
    depth, _, cols = signal_ref.shape
    zero = jnp.zeros((SUBLANES, LANES), jnp.float32)
    for group in groups(cols, WIDTH):

        def step(i, suffix, group=group):
            suffix = list(suffix)
            start = depth - (i + 1) * BATCH
            results = []
            for k in reversed([start + q for q in range(BATCH)]):
                for j, c in enumerate(group):
                    suffix[j] = suffix[j] + signal_ref[k, :, c]
                    results.append((k, c, suffix[j] * beta))
            for k, c, value in results:
                const_ref[k, :, c] = value
            return suffix

        lax.fori_loop(0, depth // BATCH, step, [zero] * len(group))


def row_factors(own_ref, other_ref, limits_ref):
    squares = own_ref[...] + other_ref[...]
    return jnp.maximum(0.0, 1.0 - limits_ref[...] / jnp.sqrt(squares + 1e-06))


def spread(factor, k):
    return jnp.broadcast_to(factor[:, k : k + 1], (SUBLANES, LANES))


def sums_kernel(own_ref, other_ref, limits_ref, state_ref, minus_ref, factor_ref, totals_ref, weighted_ref, message_ref):
    depth, _, cols = state_ref.shape
    factor = row_factors(own_ref, other_ref, limits_ref)
    for k in range(depth):
        factor_ref[k] = spread(factor, k)
    zero = jnp.zeros((SUBLANES, LANES), jnp.float32)
    totals, weights = [], []
    for group in groups(cols, WIDTH):
        total, weighted = [zero] * len(group), [minus_ref[:, c] for c in group]
        for k in range(depth):
            factor = factor_ref[k]
            for j, c in enumerate(group):
                total[j] = total[j] + state_ref[k, :, c] * factor
                weighted[j] = weighted[j] + total[j]
        totals += total
        weights += weighted
    finish_sums(depth, totals, weights, totals_ref, weighted_ref, message_ref, cols)


def route_kernel(offsets, message_ref, sibling_ref, marks_ref, *out_refs):
    for c in tiles(message_ref.shape[1]):
        own, sibling = message_ref[0:1, c], sibling_ref[0:1, c]
        lower = jnp.where(marks_ref[0:1, c] > 0.0, own, sibling)
        upward = own + sibling
        weighted = message_ref[1:2, c] + sibling_ref[1:2, c]
        downward = weighted + marks_ref[1:2, c] * upward + marks_ref[2:3, c] * lower
        for k, ref in zip(offsets, out_refs):
            ref[:, c] = jnp.where(marks_ref[2 + k : 3 + k, c] > 0.0, upward, downward)


def prefix_rows(x, sublane):
    for shift in (1, 2, 4):
        x = x + jnp.where(sublane >= shift, pltpu.roll(x, shift, 0), 0.0)
    return x


def suffix_rows(x, sublane):
    for shift in (1, 2, 4):
        x = x + jnp.where(sublane < SUBLANES - shift, pltpu.roll(x, SUBLANES - shift, 0), 0.0)
    return x


def inner_kernel(alpha, chips, scaled, state_ref, const_ref, factor_ref, totals_ref, weighted_ref, message_ref,
                 sibling_ref, inner_ref, slope_ref, base_ref):
    depth, _, cols = state_ref.shape
    rows = float(depth * SUBLANES)
    cs = tiles(cols)
    chip, core = lax.axis_index("probe"), lax.axis_index("sub")
    first = (core == 0).astype(jnp.float32)
    later = (chips - 1 - chip).astype(jnp.float32) * (2.0 * rows)
    sublane = lax.broadcasted_iota(jnp.int32, (SUBLANES, LANES), 0)
    weights = row_weights() * float(depth)

    zero = jnp.zeros((SUBLANES, LANES), jnp.float32)
    for group in groups(cols, WIDTH):
        running, double = [totals_ref[:, c] * alpha for c in group], [zero] * len(group)
        for start in reversed(range(0, depth, BATCH)):
            results = []
            for k in reversed(range(start, start + BATCH)):
                factor = factor_ref[k] if scaled else None
                for j, c in enumerate(group):
                    jump = inner_ref[k, :, c]
                    if scaled:
                        jump = jump * factor
                    double[j] = double[j] + running[j]
                    results.append((k, c, jump + const_ref[k, :, c] - double[j]))
                    running[j] = running[j] - jump * alpha
            for k, c, value in results:
                inner_ref[k, :, c] = value

    for c in cs:
        total = totals_ref[:, c]
        before = jnp.where(sublane >= 1, pltpu.roll(prefix_rows(total, sublane), 1, 0), 0.0)
        chunk = before * float(depth) + weighted_ref[:, c]
        after = jnp.where(
            sublane < SUBLANES - 1, pltpu.roll(suffix_rows(chunk, sublane), SUBLANES - 1, 0), 0.0
        )
        own, sibling = message_ref[0:1, c], sibling_ref[0:1, c]
        lower = first * own + (1.0 - first) * sibling
        shift = (1.0 - first) * lower
        base = later * (own + sibling) + first * (rows * lower + sibling_ref[1:2, c])
        slope_ref[:, c] = alpha * (before + shift)
        base_ref[:, c] = alpha * (after + base + weights * shift)


def outer_kernel(alpha, chips, offsets, inner_ref, slope_ref, base_ref, *refs):
    received, (state_ref, squares_ref) = refs[: len(offsets)], refs[len(offsets) :]
    depth, _, cols = inner_ref.shape
    rows = float(depth * SUBLANES)
    chip, core = lax.axis_index("probe"), lax.axis_index("sub")
    later = (chips - 1 - chip).astype(jnp.float32) * (2.0 * rows) + (core == 0).astype(jnp.float32) * rows
    weights = row_weights() * float(depth) + later
    earlier = [(jnp.bitwise_xor(chip, k) < chip).astype(jnp.float32) for k in offsets]

    lane = lax.broadcasted_iota(jnp.int32, (SUBLANES, LANES), 1) % depth
    sums = [jnp.zeros((SUBLANES, LANES), jnp.float32)] * 4
    for group in groups(cols, WIDTH):
        slope, value = [], []
        for c in group:
            above = sum(e * ref[:, c] for e, ref in zip(earlier, received))
            below = sum((1.0 - e) * ref[:, c] for e, ref in zip(earlier, received))
            above, below = above * alpha, below * alpha
            slope.append(slope_ref[:, c] + above)
            value.append(base_ref[:, c] + below + weights * above + slope[-1])

        for k in reversed(range(depth)):
            squares = []
            for j, c in enumerate(group):
                stepped = state_ref[k, :, c] - value[j]
                value[j] = value[j] + slope[j]
                state_ref[k, :, c] = stepped
                squares.append(stepped * stepped)
            while len(squares) > 1:
                squares = [a + b for a, b in zip(squares[::2], squares[1::2])]
            total = jnp.broadcast_to(jnp.sum(squares[0], axis=1, keepdims=True), (SUBLANES, LANES))
            sums[k % 4] = sums[k % 4] + jnp.where(lane == k, total, 0.0)
    squares_ref[...] = (sums[0] + sums[1]) + (sums[2] + sums[3])


def end_kernel(cuts, own_ref, other_ref, limits_ref, state_ref, out_hbm, jumps_ref, sems):
    depth, _, cols = state_ref.shape
    factor = row_factors(own_ref, other_ref, limits_ref)
    copies = []
    for part in range(len(cuts) - 1):
        low, high = cuts[part], cuts[part + 1]
        for start in range(low, high, BATCH):
            rows = [(k, spread(factor, k)) for k in range(start, start + BATCH)]
            for group in groups(cols, WIDTH):
                results = [(k, c, state_ref[k, :, c] * row) for k, row in rows for c in group]
                for k, c, value in results:
                    jumps_ref[k, :, c] = value
        for s in range(SUBLANES):
            copy = pltpu.make_async_copy(
                jumps_ref.at[pl.ds(low, high - low), s, :], out_hbm.at[pl.ds(s * depth + low, high - low), :],
                sems.at[part, s],
            )
            copy.start()
            copies.append(copy)
    for copy in copies:
        copy.wait()


def vmem(*shape):
    return pltpu.VMEM(shape, jnp.float32)


def call(kernel, name, operands, outs, kept=(), scratch=(), aliases=None, hbm=(), hbm_out=False):
    in_vmem = pl.BlockSpec(memory_space=pltpu.VMEM)
    in_hbm = pl.BlockSpec(memory_space=pltpu.HBM)
    operands = [
        pltpu.with_memory_space_constraint(x, pltpu.VMEM if i in kept else pltpu.HBM) if i in kept or i in hbm else x
        for i, x in enumerate(operands)
    ]
    return pl.pallas_call(
        kernel,
        out_shape=outs,
        in_specs=[in_hbm if i in hbm else in_vmem for i in range(len(operands))],
        out_specs=in_hbm if hbm_out else [in_vmem] * len(outs),
        scratch_shapes=scratch,
        input_output_aliases=aliases or {},
        compiler_params=pltpu.CompilerParams(vmem_limit_bytes=VMEM_LIMIT),
        name=name,
    )(*operands)


def local(mesh, signal, jump_sizes, thresholds):
    rows, cols = signal.shape
    chips, cores, halves = mesh.shape["probe"], mesh.shape["sub"], mesh.shape["prof"]
    depth = rows // SUBLANES
    count = float(rows * chips * cores)
    alpha, beta = STEP_LENGTH / (count * count), STEP_LENGTH / count
    offsets = tuple(reversed(range(1, chips)))
    swap = [(0, 1), (1, 0)]
    routes = {
        k: [(z * 2 + c, (z ^ k) * 2 + 1 - c) for z in range(chips) for c in range(2)] for k in offsets
    }

    block = vmem(depth, SUBLANES, cols)
    strip, line, pair = vmem(SUBLANES, cols), vmem(SUBLANES, LANES), vmem(2, cols)
    factors = vmem(depth, SUBLANES, LANES)
    begin_cuts = (0, depth // 4 * 3, depth)
    end_cuts = tuple(depth // 8 * i for i in (0, 1, 3, 5, 8))

    state, signals, minus, totals, weighted, message, limits, marks = call(
        functools.partial(begin_kernel, chips, count, begin_cuts), "begin",
        [signal, jump_sizes, thresholds.reshape(1, rows)],
        [block, block, strip, strip, strip, pair, line, vmem(chips + 2, cols)], hbm=(0, 1, 2),
        scratch=[
            vmem(1, rows), pltpu.SemaphoreType.DMA((len(begin_cuts) - 1, 2, SUBLANES)), pltpu.SemaphoreType.DMA
        ],
    )
    (const,) = call(functools.partial(suffix_kernel, beta), "suffix", [signals], [block], kept=(0,), aliases={0: 0})
    factor = None
    for iteration in range(ITERS):
        if iteration:
            factor, totals, weighted, message = call(
                sums_kernel, "sums", [own, other, limits, state, minus], [factors, strip, strip, pair], kept=(3, 4)
            )
        sibling = lax.ppermute(message, "sub", swap)
        routed = call(
            functools.partial(route_kernel, offsets), "route", [message, sibling, marks], [vmem(1, cols)] * len(offsets)
        )
        received = [lax.ppermute(x, ("probe", "sub"), routes[k]) for k, x in zip(offsets, routed)]
        scaled = factor is not None
        inner, slope, base = call(
            functools.partial(inner_kernel, alpha, chips, scaled), "inner",
            [state, const, factor if scaled else minus, totals, weighted, message, sibling],
            [block, strip, strip], kept=(0, 1, 2, 3, 4), aliases={0: 0},
        )
        state, own = call(
            functools.partial(outer_kernel, alpha, chips, offsets), "outer", [inner, slope, base, *received],
            [block, line], kept=(0, 1, 2), aliases={0: 0},
        )
        if halves == 2:
            other = lax.ppermute(own, "prof", swap)
        else:
            own, other = lax.psum(own, "prof"), jnp.zeros_like(own)
    return call(
        functools.partial(end_kernel, end_cuts), "finish", [own, other, limits, state], jax.ShapeDtypeStruct((rows, cols), jnp.float32), kept=(3,),
        hbm_out=True,
        scratch=[block, pltpu.SemaphoreType.DMA((len(end_cuts) - 1, SUBLANES))],
    )


def solution(mesh):
    spec = P(("grp", "probe", "sub"), "prof")
    return jax.shard_map(
        functools.partial(local, mesh),
        mesh=mesh,
        in_specs=(spec, spec, P(("grp", "probe", "sub"))),
        out_specs=spec,
        check_vma=False,
    )
```
